512 devices in a mesh: row: 64 (over z, x, core), col: 8 (over y).
Axes of the slice: x: 4, y: 8, z: 8, core: 2. Of those that a mesh axis runs over, the one named last changes fastest.
Arguments:
- features: bfloat16 [512, 256, 384], P('row', 'col'), may hold values from -6 to 6
- depth_weight: float32 [7, 7, 384], replicated, may hold values from -0.875 to 0.875
- depth_bias: float32 [384], replicated, may hold values from -3 to 3
- norm_gain: float32 [384], replicated, may hold values from 0.25 to 1.75
- norm_bias: float32 [384], replicated, may hold values from -2 to 2
- expand_weight: bfloat16 [384, 1536], replicated, may hold values from -0.3125 to 0.3125
- expand_bias: float32 [1536], replicated, may hold values from -3 to 3
- shrink_weight: bfloat16 [1536, 384], replicated, may hold values from -0.15625 to 0.15625
- shrink_bias: float32 [384], replicated, may hold values from -3 to 3
- layer_scale: float32 [384], replicated, may hold values from 0.3 to 3
- key_weight: bfloat16 [384, 384], replicated, may hold values from -0.3125 to 0.3125
- value_weight: bfloat16 [384, 384], replicated, may hold values from -0.3125 to 0.3125
- queries: bfloat16 [64, 384], replicated, may hold values from -192 to 192
- class_weight: float32 [384, 16], replicated, may hold values from -0.109375 to 0.109375
- tissue: int32 [64, 32], P('row', 'col'), may hold values from 0 to 1, as said below
- slide_label: int32 [16], replicated, may hold values from 0 to 1
Outputs:
- block_out: bfloat16 [512, 256, 384], P('row', 'col')
- pooled: float32 [64, 384], replicated
- slide_loss: float32 [1], replicated
The draws below stay inside these ranges and needn't reach their ends.
Inputs may be any that keep to these rules, and one draw needn't show every extreme that they name: 0 or 1; tissue[0, 0] is 1.
All inputs are finite; a program needn't handle non-finite values.
Results may differ from the reference program's by a relative error of at most 0.028.
The reference program's roundings to bfloat16 on the way (of `normed`, `hidden` and `rounded`) count: a program that leaves them out, or rounds other values in their place, can miss the bound.
Values may be sent and summed in bfloat16 or wider, within the bound.
No kernel may reach another device: no remote copies, remote signals or barrier semaphores. Data moves between devices by JAX's collectives and lax.ppermute only.
A program may use at most 128 MiB of HBM per device.

```python
import math
import jax
import jax.numpy as jnp
from jax import lax

C = 384
HID = 1536
NH = 8
NQ = 64
NLAB = 16
TILE = 8
CH = 8
HT = 512
WT = 256
NTR = 64
NTC = 32
N_ROW = 64


def draw_tissue(key, part):
    rolls = jax.random.randint(key, (NTR, NTC), 0, 100)
    bands = jnp.arange(NTR, dtype=jnp.int32)[:, None]
    limits = 20 + 70 * bands // NTR
    drawn = (rolls < limits).astype(jnp.int32)
    return drawn.at[0, 0].set(1)


def draw_queries(key, part):
    key_order = jax.random.fold_in(key, 11)
    key_entry = jax.random.fold_in(key, 12)
    order = jax.random.permutation(key_order, NQ).astype(jnp.float32)
    gains = jnp.exp(order * (jnp.log(48.0) / (NQ - 1)))
    entries = jnp.clip(jax.random.normal(key_entry, (NQ, C), jnp.float32), -4.0, 4.0)
    return (entries * gains[:, None]).astype(jnp.bfloat16)


def set_ends(values, stream_key, least, top_value):
    extent = values.shape
    place = [jax.random.randint(jax.random.fold_in(stream_key, axis), (), 0, extent[axis]) for axis in range(len(extent))]
    values = values.at[tuple(place)].set(least)
    longest = extent.index(max(extent))
    place[longest] = (place[longest] + 1) % extent[longest]
    return values.at[tuple(place)].set(top_value)


def block_levels(stream_key, extent, split, low, high):
    level, own = 1.0, jax.random.fold_in(stream_key, 6)
    for dim, parts in split:
        draws = jnp.exp(jax.random.uniform(jax.random.fold_in(own, dim), (parts,), jnp.float32, low / len(split), high / len(split)))
        level = level * jnp.repeat(draws, extent[dim] // parts).reshape([-1 if axis == dim else 1 for axis in range(len(extent))])
    return level


def bell_draw(rng, dims, spread, reach, cuts=(), held_as=jnp.bfloat16):
    level = block_levels(rng, dims, cuts, -0.22, 0.18) if cuts else 1.0
    result = jax.random.normal(rng, dims, jnp.float32) * spread * level
    return jnp.minimum(jnp.maximum(result, -reach), reach).astype(held_as)


def setup_inputs(seed: int = 0) -> dict:
    arg_keys = jax.random.split(jax.random.key(seed), 17)
    return {
        "features": bell_draw(arg_keys[0], (HT, WT, C), 1.0, 6.0, ((0, 64), (1, 8))),
        "depth_weight": bell_draw(arg_keys[1], (7, 7, C), 49 ** -0.5, 0.875, (), jnp.float32),
        "depth_bias": bell_draw(arg_keys[2], (C,), 0.5, 3.0, (), jnp.float32),
        "norm_gain": jnp.clip(1.0 + 0.15 * jax.random.normal(arg_keys[3], (C,), jnp.float32), 0.25, 1.75),
        "norm_bias": bell_draw(arg_keys[4], (C,), 0.3, 2.0, (), jnp.float32),
        "expand_weight": bell_draw(arg_keys[5], (C, HID), C ** -0.5, 0.3125),
        "expand_bias": bell_draw(arg_keys[6], (HID,), 0.5, 3.0, (), jnp.float32),
        "shrink_weight": bell_draw(arg_keys[7], (HID, C), HID ** -0.5, 0.15625),
        "shrink_bias": bell_draw(arg_keys[8], (C,), 0.5, 3.0, (), jnp.float32),
        "layer_scale": jnp.clip(jnp.exp(jax.random.uniform(arg_keys[9], (C,), jnp.float32, math.log(0.3), math.log(3.0))), 0.3, 3.0),
        "key_weight": bell_draw(arg_keys[10], (C, C), C ** -0.5, 0.3125),
        "value_weight": bell_draw(arg_keys[11], (C, C), C ** -0.5, 0.3125),
        "queries": draw_queries(jax.random.fold_in(arg_keys[16], 71), 0),
        "class_weight": bell_draw(arg_keys[13], (C, NLAB), (NQ * C // 8) ** -0.5, 0.109375, (), jnp.float32),
        "tissue": draw_tissue(jax.random.fold_in(arg_keys[16], 71), 0),
        "slide_label": set_ends(jax.random.randint(arg_keys[15], (NLAB,), 0, 2), jax.random.fold_in(arg_keys[15], 1), 0, 1).astype(jnp.int32),
    }


def spread_heads(scale, width):
    return jnp.repeat(jnp.transpose(scale), width // scale.shape[0], axis=1)

def band_work(band, padded, features, tissue, depth_weight, depth_bias, norm_gain, norm_bias, expand_weight, expand_bias, shrink_weight, shrink_bias, layer_scale, key_weight, value_weight, queries):
    start = (band * CH).astype(jnp.int32)
    window = lax.dynamic_slice_in_dim(padded, start, CH + 6, 0)
    conv = jnp.zeros((CH, WT, C), jnp.float32) + depth_bias
    for offset_row in range(7):
        for offset_col in range(7):
            conv = conv + window[offset_row:offset_row + CH, offset_col:offset_col + WT].astype(jnp.float32) * depth_weight[offset_row, offset_col]
    center = lax.optimization_barrier(jnp.mean(conv, axis=-1, keepdims=True))
    variance = lax.optimization_barrier(jnp.mean((conv - center) ** 2, axis=-1, keepdims=True))
    normed = ((conv - center) * lax.rsqrt(variance + 1e-06) * norm_gain + norm_bias).astype(jnp.bfloat16)
    expanded = jnp.dot(normed.reshape(CH * WT, C), expand_weight, preferred_element_type=jnp.float32) + expand_bias
    hidden = jax.nn.gelu(expanded, approximate=False).astype(jnp.bfloat16)
    shrunk = jnp.dot(hidden, shrink_weight, preferred_element_type=jnp.float32) + shrink_bias
    inputs = lax.dynamic_slice_in_dim(features, start, CH, 0).reshape(CH * WT, C)
    block_out = (inputs.astype(jnp.float32) + layer_scale * shrunk).astype(jnp.bfloat16)
    keys = jnp.dot(block_out, key_weight, preferred_element_type=jnp.float32).astype(jnp.bfloat16)
    values = jnp.dot(block_out, value_weight, preferred_element_type=jnp.float32).astype(jnp.bfloat16)
    tile_rows = lax.dynamic_slice_in_dim(tissue, (band * (CH // TILE)).astype(jnp.int32), CH // TILE, 0)
    live_cells = jnp.repeat(jnp.repeat(tile_rows, TILE, axis=0), TILE, axis=1).reshape(CH * WT) > 0
    size = C // NH
    query_heads = queries.astype(jnp.float32).reshape(NQ, NH, size)
    key_heads = keys.astype(jnp.float32).reshape(CH * WT, NH, size)
    scores = jnp.einsum('qhd,nhd->hqn', query_heads, key_heads) * size ** (-0.5)
    live = live_cells[None, None, :]
    scores = jnp.where(live, scores, -1e+30)
    peak = lax.optimization_barrier(jnp.max(scores, axis=2))
    weights = jnp.where(live, jnp.exp(scores - peak[:, :, None]), 0.0)
    total = lax.optimization_barrier(jnp.sum(weights, axis=2))
    rounded = weights.astype(jnp.bfloat16)
    weighted = jnp.einsum('hqn,nhd->qhd', rounded.astype(jnp.float32), values.astype(jnp.float32).reshape(CH * WT, NH, size)).reshape(NQ, C)
    return (block_out.reshape(CH, WT, C), peak, total, weighted)

def reference(features, depth_weight, depth_bias, norm_gain, norm_bias, expand_weight, expand_bias, shrink_weight, shrink_bias, layer_scale, key_weight, value_weight, queries, class_weight, tissue, slide_label):
    padded = jnp.pad(features, ((3, 3), (3, 3), (0, 0)))

    def one_band(band):
        return band_work(band, padded, features, tissue, depth_weight, depth_bias, norm_gain, norm_bias, expand_weight, expand_bias, shrink_weight, shrink_bias, layer_scale, key_weight, value_weight, queries)
    bands, peaks, totals, weighted = lax.map(one_band, jnp.arange(N_ROW, dtype=jnp.int32))
    block_out = bands.reshape(HT, WT, C)
    peak = lax.optimization_barrier(jnp.max(peaks, axis=0))
    factors = jnp.exp(peaks - peak[None])
    total = lax.optimization_barrier(jnp.sum(totals * factors, axis=0))
    summed = jnp.zeros((NQ, C), jnp.float32)
    for band in range(N_ROW):
        summed = summed + weighted[band] * spread_heads(factors[band], C)
    pooled = summed / spread_heads(total, C)
    logits = lax.optimization_barrier(jnp.sum(jnp.dot(pooled, class_weight, precision=lax.Precision.HIGHEST), axis=0))
    slide_loss = jnp.sum(jax.nn.softplus(logits) - slide_label.astype(jnp.float32) * logits).reshape(1)
    return (block_out, pooled, slide_loss)
```

```python
import jax
import jax.numpy as jnp
from jax import lax
from jax.sharding import PartitionSpec as P

NH = 8
NQ = 64
TILE = 8
LOG2E = 1.4426950408889634
NEAR = [[z * 8 + r for r in range(8)] for z in range(8)]
FAR = [[z * 8 + r for z in range(8)] for r in range(8)]


def with_halo(block, sides, width):
    for axis, dim in sides:
        count = lax.axis_size(axis)
        forward = [(i, i + 1) for i in range(count - 1)]
        backward = [(target, source) for source, target in forward]
        low = lax.ppermute(
            lax.slice_in_dim(block, block.shape[dim] - width, None, axis=dim), axis, forward
        )
        high = lax.ppermute(lax.slice_in_dim(block, 0, width, axis=dim), axis, backward)
        block = jnp.concatenate([low, block, high], axis=dim)
    return block


def head_spread(width):
    size = width // NH
    head = lax.broadcasted_iota(jnp.int32, (NH, width), 0)
    channel = lax.broadcasted_iota(jnp.int32, (NH, width), 1)
    return (channel // size == head).astype(jnp.bfloat16)


def combined(parts, width):
    exponent = parts[:, :, width : width + NH]
    total = parts[:, :, width + NH : width + 2 * NH]
    top = jnp.max(exponent, axis=0)
    factor = jnp.exp2(exponent - top)
    total = jnp.sum(total * factor, axis=0)
    n, q = factor.shape[:2]
    spread = jnp.dot(
        factor.reshape(n * q, NH).astype(jnp.bfloat16),
        head_spread(width),
        preferred_element_type=jnp.float32,
    ).reshape(n, q, width)
    weighted = jnp.sum(parts[:, :, :width] * spread, axis=0)
    return weighted, top, total


def packed(weighted, top, total):
    q = weighted.shape[0]
    return jnp.concatenate(
        [weighted, top, total, jnp.zeros((q, 128 - 2 * NH), jnp.float32)], axis=1
    )


def everyone(part, axis, groups=None):
    return lax.all_to_all(
        jnp.broadcast_to(part[None], (8,) + part.shape), axis, 0, 0, axis_index_groups=groups, tiled=True
    )


def merged(weighted, top, total):
    width = weighted.shape[1]
    rows = packed(weighted, top, total).reshape(8, NQ // 8, width + 128)
    share = lax.all_to_all(rows, "row", 0, 0, axis_index_groups=NEAR, tiled=True)
    part = packed(*combined(share, width))
    part = packed(*combined(everyone(part, "row", FAR), width))
    weighted, top, total = combined(everyone(part, "col"), width)
    inverse = jnp.dot(
        1.0 / total, head_spread(width).astype(jnp.float32), precision=lax.Precision.HIGHEST
    )
    pooled = everyone(weighted * inverse, "row", NEAR)
    return pooled.reshape(NQ, width)


def per_device(
    features,
    depth_weight,
    depth_bias,
    norm_gain,
    norm_bias,
    expand_weight,
    expand_bias,
    shrink_weight,
    shrink_bias,
    layer_scale,
    key_weight,
    value_weight,
    queries,
    class_weight,
    tissue,
    slide_label,
):
    rows, cols, width = features.shape
    padded = with_halo(features, (("row", 0), ("col", 1)), 3)
    conv = jnp.zeros((rows, cols, width), jnp.float32) + depth_bias
    for offset_row in range(7):
        for offset_col in range(7):
            conv = (
                conv
                + padded[offset_row : offset_row + rows, offset_col : offset_col + cols].astype(
                    jnp.float32
                )
                * depth_weight[offset_row, offset_col]
            )
    center = jnp.mean(conv, axis=-1, keepdims=True)
    variance = jnp.mean((conv - center) ** 2, axis=-1, keepdims=True)
    normed = ((conv - center) * lax.rsqrt(variance + 1e-06) * norm_gain + norm_bias).astype(
        jnp.bfloat16
    )
    count = rows * cols
    expanded = (
        jnp.dot(normed.reshape(count, width), expand_weight, preferred_element_type=jnp.float32)
        + expand_bias
    )
    hidden = jax.nn.gelu(expanded, approximate=False).astype(jnp.bfloat16)
    shrunk = jnp.dot(hidden, shrink_weight, preferred_element_type=jnp.float32) + shrink_bias
    block_flat = (features.reshape(count, width).astype(jnp.float32) + layer_scale * shrunk).astype(
        jnp.bfloat16
    )
    keys = jnp.dot(block_flat, key_weight, preferred_element_type=jnp.float32).astype(jnp.bfloat16)
    values = jnp.dot(block_flat, value_weight, preferred_element_type=jnp.float32).astype(
        jnp.bfloat16
    )
    live_cells = jnp.repeat(jnp.repeat(tissue, TILE, axis=0), TILE, axis=1).reshape(count) > 0
    size = width // NH
    scores = jnp.einsum(
        "qhd,nhd->hqn",
        queries.reshape(NQ, NH, size),
        keys.reshape(count, NH, size),
        preferred_element_type=jnp.float32,
    ) * (size ** (-0.5) * LOG2E)
    live = live_cells[None, None, :]
    scores = jnp.where(live, scores, -1e30)
    top = jnp.ceil(jnp.max(scores, axis=2))
    weights = jnp.where(live, jnp.exp2(scores - top[:, :, None]), 0.0)
    total = jnp.sum(weights, axis=2)
    rounded = weights.astype(jnp.bfloat16)
    weighted = jnp.einsum(
        "hqn,nhd->qhd", rounded, values.reshape(count, NH, size), preferred_element_type=jnp.float32
    ).reshape(NQ, width)
    pooled = merged(weighted, top.T, total.T)
    logits = jnp.sum(jnp.dot(pooled, class_weight, precision=lax.Precision.HIGHEST), axis=0)
    slide_loss = jnp.sum(
        jax.nn.softplus(logits) - slide_label.astype(jnp.float32) * logits
    ).reshape(1)
    return (block_flat.reshape(rows, cols, width), pooled, slide_loss)


def solution(mesh):
    placed = (P("row", "col", None),) + (P(),) * 13 + (P("row", "col"), P())
    return jax.shard_map(
        per_device,
        mesh=mesh,
        in_specs=placed,
        out_specs=(P("row", "col", None), P(), P()),
        check_vma=False,
    )
```

```python
import jax
import jax.numpy as jnp
from jax import lax
from jax.experimental import pallas as pl
from jax.experimental.pallas import tpu as pltpu
from jax.sharding import PartitionSpec as P

NH = 8
NQ = 64
TILE = 8
LOG2E = 1.4426950408889634
NEAR = [[z * 8 + r for r in range(8)] for z in range(8)]
FAR = [[z * 8 + r for z in range(8)] for r in range(8)]


WIDTH = 384
LANES = 128
CELLS_R = 8
CELLS_C = 32
HID = 1536


def taps(acc, rows, weight_ref, lanes, b, first):
    for a in range(7):
        weight = weight_ref[a, b : b + 1, lanes]
        for i in range(CELLS_R):
            at = i + a - 3 - first
            if 0 <= at < len(rows):
                acc[i] = acc[i] + rows[at] * weight
    return acc


def own_kernel(
    x_hbm,
    weight_hbm,
    expand_hbm,
    shrink_hbm,
    key_hbm,
    value_hbm,
    query_hbm,
    bias_hbm,
    gain_hbm,
    norm_bias_hbm,
    shrink_bias_hbm,
    scale_hbm,
    expand_bias_hbm,
    acc_ref,
    first_ref,
    last_ref,
    x_ref,
    weight_ref,
    expand_ref,
    shrink_ref,
    key_ref,
    turned_ref,
    big_ref,
    rows_ref,
    wide,
    value_ref,
    query_ref,
    bias_ref,
    gain_ref,
    norm_bias_ref,
    shrink_bias_ref,
    scale_ref,
    expand_bias_ref,
    sems,
):
    pairs = (
        (x_hbm, x_ref),
        (weight_hbm, weight_ref),
        (bias_hbm, bias_ref),
        (query_hbm, query_ref),
        (value_hbm, value_ref),
        (gain_hbm, gain_ref),
        (norm_bias_hbm, norm_bias_ref),
        (shrink_bias_hbm, shrink_bias_ref),
        (scale_hbm, scale_ref),
        (expand_bias_hbm, expand_bias_ref),
        (key_hbm, key_ref),
        (expand_hbm, expand_ref),
        (shrink_hbm, shrink_ref),
    )
    copies = [pltpu.make_async_copy(s, d, sems.at[k]) for k, (s, d) in enumerate(pairs)]
    for copy in copies:
        copy.start()
    for copy in copies[:3]:
        copy.wait()
    rows_ref[8:9, :] = bias_ref[...].reshape(1, WIDTH)
    first_ref[...] = x_ref[:, 0:3, :]
    last_ref[...] = x_ref[:, CELLS_C - 3 : CELLS_C, :]
    for c in range(3):
        lanes = pl.ds(c * LANES, LANES)
        wide[c, :, 0:8, :] = jnp.zeros((CELLS_R, 8, LANES), jnp.float32)
        wide[c, :, 8 + CELLS_C : 16 + CELLS_C, :] = jnp.zeros((CELLS_R, 8, LANES), jnp.float32)
        wide[c, :, 8 : 8 + CELLS_C, :] = x_ref[:, :, lanes].astype(jnp.float32)

    def lane_tile(c, carry):
        lanes = pl.ds(pl.multiple_of(c * LANES, LANES), LANES)
        bias = jnp.broadcast_to(rows_ref[8:9, lanes], (8, LANES))
        for j in range(CELLS_C // 8):
            acc = [bias] * CELLS_R
            for b in range(7):
                at = 8 * j + 5 + b
                rows = [wide[c, r, at : at + 8, :] for r in range(CELLS_R)]
                acc = taps(acc, rows, weight_ref, lanes, b, 0)
            for i in range(CELLS_R):
                acc_ref[i, 8 * j : 8 * j + 8, lanes] = acc[i]
        return carry

    lax.fori_loop(0, 3, lane_tile, 0)
    for copy in copies[3:]:
        copy.wait()
    for row, ref in enumerate((gain_ref, norm_bias_ref, shrink_bias_ref, scale_ref)):
        rows_ref[row : row + 1, :] = ref[...].reshape(1, WIDTH)
    for k in range(HID // WIDTH):
        rows_ref[4 + k : 5 + k, :] = expand_bias_ref[k * WIDTH : (k + 1) * WIDTH].reshape(1, WIDTH)
    turned_ref[...] = value_ref[...].astype(jnp.float32).T.astype(jnp.bfloat16)
    query = query_ref[...].astype(jnp.float32)
    query = jnp.concatenate([query, query], axis=0).T
    head = lax.broadcasted_iota(jnp.int32, (WIDTH, LANES), 0) // (WIDTH // NH)
    half = lax.broadcasted_iota(jnp.int32, (WIDTH, LANES), 1) // NQ
    for t in range(NH // 2):
        big_ref[:, t * LANES : (t + 1) * LANES] = jnp.where(
            head == 2 * t + half, query, 0.0
        ).astype(jnp.bfloat16)


def rows_kernel(acc_in, low_ref, high_ref, weight_ref, acc_ref, wide):
    for c in range(3):
        lanes = pl.ds(c * LANES, LANES)
        wide[c, :, 0:8, :] = jnp.zeros((6, 8, LANES), jnp.float32)
        wide[c, :, 8 + CELLS_C : 16 + CELLS_C, :] = jnp.zeros((6, 8, LANES), jnp.float32)
        wide[c, 0:3, 8 : 8 + CELLS_C, :] = low_ref[:, :, lanes].astype(jnp.float32)
        wide[c, 3:6, 8 : 8 + CELLS_C, :] = high_ref[:, :, lanes].astype(jnp.float32)

    def lane_tile(c, carry):
        lanes = pl.ds(pl.multiple_of(c * LANES, LANES), LANES)
        for j in range(CELLS_C // 8):
            acc = [acc_in[i, 8 * j : 8 * j + 8, lanes] for i in range(CELLS_R)]
            for b in range(7):
                at = 8 * j + 5 + b
                rows = [wide[c, r, at : at + 8, :] for r in range(6)]
                acc = taps(acc, rows[:3], weight_ref, lanes, b, -3)
                acc = taps(acc, rows[3:], weight_ref, lanes, b, CELLS_R)
            for i in range(CELLS_R):
                acc_ref[i, 8 * j : 8 * j + 8, lanes] = acc[i]
        return carry

    lax.fori_loop(0, 3, lane_tile, 0)


def gelu(x):
    return 0.5 * x * (1.0 + lax.erf(x * (0.5**0.5)))


def marked(weighted, marks):
    high = marks.astype(jnp.bfloat16).astype(jnp.float32)
    rest = marks - high
    middle = rest.astype(jnp.bfloat16).astype(jnp.float32)
    low = (rest - middle).astype(jnp.bfloat16).astype(jnp.float32)
    marks = high + pltpu.roll(middle, NH, 1) + pltpu.roll(low, 2 * NH, 1)
    return jnp.concatenate([weighted, marks], axis=1).astype(jnp.bfloat16)


def cells_kernel(
    tissue_ref,
    acc_ref,
    left_ref,
    right_ref,
    weight_ref,
    x_ref,
    rows_ref,
    expand_ref,
    shrink_ref,
    key_ref,
    turned_ref,
    big_ref,
    out_ref,
    part_ref,
    edge,
    normed,
    hidden,
    sums,
):
    count = CELLS_R * CELLS_C
    tall = CELLS_R + 6
    edge[...] = jnp.zeros(edge.shape, jnp.float32)
    for c in range(3):
        lanes = pl.ds(c * LANES, LANES)
        edge[0, c, :, 5:8, :] = left_ref[:, :, lanes].astype(jnp.float32)
        edge[1, c, :, 8:11, :] = right_ref[:, :, lanes].astype(jnp.float32)

    def lane_tile(c, carry):
        lanes = pl.ds(pl.multiple_of(c * LANES, LANES), LANES)
        for side, j in ((0, 0), (1, CELLS_C // 8 - 1)):
            acc = [acc_ref[i, 8 * j : 8 * j + 8, lanes] for i in range(CELLS_R)]
            for b in (0, 1, 2) if side == 0 else (4, 5, 6):
                at = 5 + b if side == 0 else b - 3
                rows = [edge[side, c, r, at : at + 8, :] for r in range(tall)]
                acc = taps(acc, rows, weight_ref, lanes, b, -3)
            for i in range(CELLS_R):
                acc_ref[i, 8 * j : 8 * j + 8, lanes] = acc[i]
        return carry

    lax.fori_loop(0, 3, lane_tile, 0)
    gain, norm_bias, shrink_bias, scale = (rows_ref[k : k + 1, :] for k in range(4))
    for i in range(CELLS_R):
        conv = acc_ref[i]
        center = jnp.mean(conv, axis=-1, keepdims=True)
        conv = conv - center
        variance = jnp.mean(conv * conv, axis=-1, keepdims=True)
        normed[i * CELLS_C : (i + 1) * CELLS_C, :] = (
            conv * lax.rsqrt(variance + 1e-06) * gain + norm_bias
        ).astype(jnp.bfloat16)
    for k in range(HID // WIDTH):
        lanes = slice(k * WIDTH, (k + 1) * WIDTH)
        part = jnp.dot(normed[...], expand_ref[:, lanes], preferred_element_type=jnp.float32)
        hidden[:, lanes] = gelu(part + rows_ref[4 + k : 5 + k, :]).astype(jnp.bfloat16)
    shrunk = jnp.dot(hidden[...], shrink_ref[...], preferred_element_type=jnp.float32)
    shrunk = shrunk + shrink_bias
    block = (x_ref[...].reshape(count, WIDTH).astype(jnp.float32) + scale * shrunk).astype(
        jnp.bfloat16
    )
    out_ref[...] = block.reshape(CELLS_R, CELLS_C, WIDTH)
    keys = jnp.dot(block, key_ref[...], preferred_element_type=jnp.float32).astype(jnp.bfloat16)
    values = lax.dot_general(
        turned_ref[...], block, (((1,), (1,)), ((), ())), preferred_element_type=jnp.float32
    ).astype(jnp.bfloat16)
    size = WIDTH // NH
    groups = CELLS_C // TILE
    line = lax.broadcasted_iota(jnp.int32, (NH, LANES), 0)
    tops = jnp.zeros((NH, LANES), jnp.float32)
    totals = jnp.zeros((NH, LANES), jnp.float32)
    for t in range(NH // 2):
        scores = jnp.dot(
            keys, big_ref[:, t * LANES : (t + 1) * LANES], preferred_element_type=jnp.float32
        ) * (size**-0.5 * LOG2E)
        scores = scores.reshape(CELLS_R, groups, TILE, LANES)
        scores = [jnp.where(tissue_ref[0, g] > 0, scores[:, g], -1e30) for g in range(groups)]
        top = scores[0]
        for g in range(1, groups):
            top = jnp.maximum(top, scores[g])
        top = jnp.ceil(jnp.max(jnp.max(top, axis=0), axis=0, keepdims=True))
        weights = [
            jnp.where(tissue_ref[0, g] > 0, jnp.exp2(scores[g] - top), 0.0) for g in range(groups)
        ]
        total = weights[0]
        for g in range(1, groups):
            total = total + weights[g]
        total = jnp.sum(jnp.sum(total, axis=0), axis=0, keepdims=True)
        weights = jnp.stack(weights, axis=1).reshape(count, LANES).astype(jnp.bfloat16)
        pair = jnp.dot(
            values[2 * size * t : 2 * size * (t + 1), :], weights, preferred_element_type=jnp.float32
        )
        sums[2 * size * t : 2 * size * t + size, :] = pair[:size]
        sums[2 * size * t + size : 2 * size * (t + 1), :] = pltpu.roll(pair[size:], NQ, 1)
        tops = jnp.where(line == 2 * t, top, tops)
        tops = jnp.where(line == 2 * t + 1, pltpu.roll(jnp.broadcast_to(top, (NH, LANES)), NQ, 1), tops)
        totals = jnp.where(line == 2 * t, total, totals)
        totals = jnp.where(
            line == 2 * t + 1, pltpu.roll(jnp.broadcast_to(total, (NH, LANES)), NQ, 1), totals
        )
    sums[WIDTH:, :] = jnp.zeros((LANES, LANES), jnp.float32)
    sums[WIDTH : WIDTH + NH, :] = tops
    sums[WIDTH + 3 * NH : WIDTH + 4 * NH, :] = totals
    part = sums[...].T
    part_ref[...] = marked(part[:NQ, :WIDTH], part[:NQ, WIDTH:])


def spread_matrix(first, copies):
    lane = lax.broadcasted_iota(jnp.int32, (LANES, WIDTH), 0) - first
    head = lax.broadcasted_iota(jnp.int32, (LANES, WIDTH), 1) // (WIDTH // NH)
    inside = (lane >= 0) & (lane < copies * NH)
    return jnp.where(inside & (lane % NH == head), 1.0, 0.0).astype(jnp.bfloat16)


def combined(parts):
    n, q = parts.shape[:2]
    parts = parts.astype(jnp.float32)
    marks = parts[:, :, WIDTH:].reshape(n * q, LANES)
    marks = marks + pltpu.roll(marks, LANES - NH, 1) + pltpu.roll(marks, LANES - 2 * NH, 1)
    top = jnp.max(marks.reshape(n, q, LANES), axis=0)
    factor = jnp.exp2(marks.reshape(n, q, LANES) - top).reshape(n * q, LANES)
    factor = factor.astype(jnp.bfloat16)
    spread = jnp.dot(factor, spread_matrix(0, 1), preferred_element_type=jnp.float32)
    weighted = jnp.sum(parts[:, :, :WIDTH] * spread.reshape(n, q, WIDTH), axis=0)
    total = marks * pltpu.roll(factor.astype(jnp.float32), 3 * NH, 1)
    total = jnp.sum(total.reshape(n, q, LANES), axis=0)
    lane = lax.broadcasted_iota(jnp.int32, (q, LANES), 1)
    inside = (lane >= 3 * NH) & (lane < 4 * NH)
    return weighted, jnp.where(lane < NH, top, 0.0), jnp.where(inside, total, 1.0), inside


def merge_kernel(parts_ref, out_ref):
    weighted, top, total, inside = combined(parts_ref[...])
    part = marked(weighted, top + jnp.where(inside, total, 0.0))
    out_ref[...] = jnp.broadcast_to(part[None], out_ref.shape)


def pool_kernel(parts_ref, out_ref):
    weighted, _, total, inside = combined(parts_ref[...])
    marks = marked(weighted, jnp.where(inside, 1.0 / total, 0.0))[:, WIDTH:]
    inverse = jnp.dot(marks, spread_matrix(3 * NH, 3), preferred_element_type=jnp.float32)
    out_ref[...] = jnp.broadcast_to((weighted * inverse)[None], out_ref.shape)


def loss_kernel(pooled_ref, class_ref, label_ref, out_ref, loss_ref):
    pooled = pooled_ref[...]
    out_ref[...] = pooled
    lines = jnp.sum(pooled.reshape(NQ // 8, 8, WIDTH), axis=0)
    logits = jnp.dot(
        lines, class_ref[...], precision=lax.Precision.HIGHEST, preferred_element_type=jnp.float32
    )
    logits = jnp.sum(logits, axis=0, keepdims=True)
    label = label_ref[...].reshape(logits.shape).astype(jnp.float32)
    soft = jnp.maximum(logits, 0.0) + jnp.log1p(jnp.exp(-jnp.abs(logits)))
    loss_ref[0] = jnp.sum(soft - label * logits)


def everyone(part, axis, groups=None):
    return lax.all_to_all(part, axis, 0, 0, axis_index_groups=groups, tiled=True)


def call(kernel, out_shape, name, *args, **more):
    return pl.pallas_call(kernel, out_shape=out_shape, name=name, **more, **params())(*args)


def merged(part, class_weight, slide_label):
    chunk = (8, NQ // 8, WIDTH + LANES)
    same = jax.ShapeDtypeStruct(chunk, jnp.bfloat16)
    parts = everyone(part.reshape(chunk), "row", NEAR)
    parts = everyone(call(merge_kernel, same, "merge_near", parts), "row", FAR)
    parts = everyone(call(merge_kernel, same, "merge_far", parts), "col")
    rows = jax.ShapeDtypeStruct((8, NQ // 8, WIDTH), jnp.float32)
    pooled = everyone(call(pool_kernel, rows, "pool", parts), "row", NEAR)
    return call(
        loss_kernel,
        (jax.ShapeDtypeStruct((NQ, WIDTH), jnp.float32), jax.ShapeDtypeStruct((1,), jnp.float32)),
        "loss",
        pooled.reshape(NQ, WIDTH),
        class_weight,
        slide_label,
        out_specs=(pl.BlockSpec(memory_space=pltpu.VMEM), pl.BlockSpec(memory_space=pltpu.SMEM)),
    )


def vmem(*shape):
    return pltpu.VMEM(shape, jnp.float32)


def params(flops=1000000):
    return dict(
        compiler_params=pltpu.CompilerParams(vmem_limit_bytes=24 * 1024 * 1024),
        cost_estimate=pl.CostEstimate(flops=flops, bytes_accessed=1000000, transcendentals=0),
    )


def exchanged(first, last, axis):
    count = lax.axis_size(axis)
    forward = [(i, i + 1) for i in range(count - 1)]
    backward = [(target, source) for source, target in forward]
    return lax.ppermute(last, axis, forward), lax.ppermute(first, axis, backward)


def per_device(
    features,
    depth_weight,
    depth_bias,
    norm_gain,
    norm_bias,
    expand_weight,
    expand_bias,
    shrink_weight,
    shrink_bias,
    layer_scale,
    key_weight,
    value_weight,
    queries,
    class_weight,
    tissue,
    slide_label,
):
    rows, cols, width = features.shape
    f32, bf16 = jnp.float32, jnp.bfloat16
    hbm, whole = pl.BlockSpec(memory_space=pltpu.HBM), pl.BlockSpec(memory_space=pltpu.VMEM)
    shaped = jax.ShapeDtypeStruct
    low, high = exchanged(features[:3], features[-3:], "row")
    acc, first, last, cells, taps_, expand, shrink, key, turned, big, lines = call(
        own_kernel,
        (
            shaped((rows, cols, width), f32),
            shaped((rows, 3, width), bf16),
            shaped((rows, 3, width), bf16),
            shaped(features.shape, bf16),
            shaped(depth_weight.shape, f32),
            shaped(expand_weight.shape, bf16),
            shaped(shrink_weight.shape, bf16),
            shaped(key_weight.shape, bf16),
            shaped(value_weight.shape, bf16),
            shaped((width, NH * NQ), bf16),
            shaped((16, width), f32),
        ),
        "own_cells",
        *(
            pltpu.with_memory_space_constraint(array, pltpu.HBM)
            for array in (
                features,
                depth_weight,
                expand_weight,
                shrink_weight,
                key_weight,
                value_weight,
                queries,
                depth_bias,
                norm_gain,
                norm_bias,
                shrink_bias,
                layer_scale,
                expand_bias,
            )
        ),
        in_specs=[hbm] * 13,
        out_specs=(whole,) * 11,
        scratch_shapes=[
            vmem(3, rows, cols + 16, LANES),
            pltpu.VMEM(value_weight.shape, bf16),
            pltpu.VMEM(queries.shape, bf16),
            *(vmem(width) for _ in range(5)),
            vmem(HID),
            pltpu.SemaphoreType.DMA((13,)),
        ],
    )
    left, right = exchanged(
        jnp.concatenate([low[:, :3], first, high[:, :3]], axis=0),
        jnp.concatenate([low[:, -3:], last, high[:, -3:]], axis=0),
        "col",
    )
    acc = call(
        rows_kernel,
        shaped((rows, cols, width), f32),
        "halo_rows",
        acc,
        low,
        high,
        taps_,
        scratch_shapes=[vmem(3, 6, cols + 16, LANES)],
        input_output_aliases={0: 0},
    )
    block_out, part = call(
        cells_kernel,
        (shaped((rows, cols, width), bf16), shaped((NQ, width + LANES), bf16)),
        "cells",
        tissue,
        acc,
        left,
        right,
        taps_,
        cells,
        lines,
        expand,
        shrink,
        key,
        turned,
        big,
        in_specs=[pl.BlockSpec(memory_space=pltpu.SMEM)] + [whole] * 11,
        scratch_shapes=[
            vmem(2, 3, rows + 6, 16, LANES),
            pltpu.VMEM((rows * cols, width), bf16),
            pltpu.VMEM((rows * cols, HID), bf16),
            vmem(width + LANES, LANES),
        ],
    )
    pooled, slide_loss = merged(part, class_weight, slide_label)
    return (block_out, pooled, slide_loss)


def solution(mesh):
    placed = (P("row", "col", None),) + (P(),) * 13 + (P("row", "col"), P())
    return jax.shard_map(
        per_device,
        mesh=mesh,
        in_specs=placed,
        out_specs=(P("row", "col", None), P(), P()),
        check_vma=False,
    )
```

```python
import jax
import jax.numpy as jnp
from jax import lax
from jax.experimental import pallas as pl
from jax.experimental.pallas import tpu as pltpu
from jax.sharding import PartitionSpec as P

NH = 8
NQ = 64
TILE = 8
LOG2E = 1.4426950408889634


def device(z, near, y):
    return (z * 8 + near) * 8 + y


EIGHT, FOUR, TWO = range(8), range(4), range(2)
FIRST = [[device(2 * z + k, n, y) for k in TWO for n in EIGHT] for z in FOUR for y in EIGHT]
SECOND = [
    [device(2 * z + k, n, 2 * y + m) for z in FOUR for y in FOUR]
    for k in TWO
    for n in EIGHT
    for m in TWO
]
THIRD = [[device(z, n, 2 * y + m) for m in TWO for n in EIGHT] for z in EIGHT for y in FOUR]


WIDTH = 384
LANES = 128
CELLS_R = 8
CELLS_C = 32
HID = 1536
HALF = 16


def taps(acc, rows, weight_ref, lanes, b, first):
    for a in range(7):
        weight = weight_ref[a, b : b + 1, lanes]
        for i in range(CELLS_R):
            at = i + a - 3 - first
            if 0 <= at < len(rows):
                acc[i] = acc[i] + rows[at] * weight
    return acc


def own_kernel(
    x_hbm,
    weight_hbm,
    expand_hbm,
    shrink_hbm,
    key_hbm,
    value_hbm,
    query_hbm,
    bias_hbm,
    gain_hbm,
    norm_bias_hbm,
    shrink_bias_hbm,
    scale_hbm,
    expand_bias_hbm,
    acc_ref,
    first_ref,
    last_ref,
    x_ref,
    weight_ref,
    expand_ref,
    shrink_ref,
    key_ref,
    turned_ref,
    big_ref,
    rows_ref,
    wide,
    value_ref,
    query_ref,
    bias_ref,
    gain_ref,
    norm_bias_ref,
    shrink_bias_ref,
    scale_ref,
    expand_bias_ref,
    sems,
):
    pairs = (
        (x_hbm, x_ref),
        (weight_hbm, weight_ref),
        (bias_hbm, bias_ref),
        (query_hbm, query_ref),
        (value_hbm, value_ref),
        (gain_hbm, gain_ref),
        (norm_bias_hbm, norm_bias_ref),
        (shrink_bias_hbm, shrink_bias_ref),
        (scale_hbm, scale_ref),
        (expand_bias_hbm, expand_bias_ref),
        (key_hbm, key_ref),
        (expand_hbm, expand_ref),
        (shrink_hbm, shrink_ref),
    )
    copies = [pltpu.make_async_copy(s, d, sems.at[k]) for k, (s, d) in enumerate(pairs)]
    for copy in copies:
        copy.start()
    for copy in copies[:3]:
        copy.wait()
    rows_ref[8:9, :] = bias_ref[...].reshape(1, WIDTH)
    first_ref[...] = x_ref[:, 0:3, :]
    last_ref[...] = x_ref[:, CELLS_C - 3 : CELLS_C, :]
    for c in range(3):
        lanes = pl.ds(c * LANES, LANES)
        wide[c, :, 0:8, :] = jnp.zeros((CELLS_R, 8, LANES), jnp.float32)
        wide[c, :, 8 + CELLS_C : 16 + CELLS_C, :] = jnp.zeros((CELLS_R, 8, LANES), jnp.float32)
        wide[c, :, 8 : 8 + CELLS_C, :] = x_ref[:, :, lanes].astype(jnp.float32)

    def lane_tile(c, carry):
        lanes = pl.ds(pl.multiple_of(c * LANES, LANES), LANES)
        bias = jnp.broadcast_to(rows_ref[8:9, lanes], (8, LANES))
        for j in range(CELLS_C // 8):
            acc = [bias] * CELLS_R
            for b in range(7):
                at = 8 * j + 5 + b
                rows = [wide[c, r, at : at + 8, :] for r in range(CELLS_R)]
                acc = taps(acc, rows, weight_ref, lanes, b, 0)
            for i in range(CELLS_R):
                acc_ref[i, 8 * j : 8 * j + 8, lanes] = acc[i]
        return carry

    lax.fori_loop(0, 3, lane_tile, 0)
    for copy in copies[3:]:
        copy.wait()
    for row, ref in enumerate((gain_ref, norm_bias_ref, shrink_bias_ref, scale_ref)):
        rows_ref[row : row + 1, :] = ref[...].reshape(1, WIDTH)
    for k in range(HID // WIDTH):
        rows_ref[4 + k : 5 + k, :] = expand_bias_ref[k * WIDTH : (k + 1) * WIDTH].reshape(1, WIDTH)
    turned_ref[...] = value_ref[...].astype(jnp.float32).T.astype(jnp.bfloat16)
    query = query_ref[...].astype(jnp.float32)
    query = jnp.concatenate([query, query], axis=0).T
    head = lax.broadcasted_iota(jnp.int32, (WIDTH, LANES), 0) // (WIDTH // NH)
    half = lax.broadcasted_iota(jnp.int32, (WIDTH, LANES), 1) // NQ
    for t in range(NH // 2):
        big_ref[:, t * LANES : (t + 1) * LANES] = jnp.where(
            head == 2 * t + half, query, 0.0
        ).astype(jnp.bfloat16)


def halo_rows(acc_in, low_ref, high_ref, weight_ref, acc_ref, wide):
    for c in range(3):
        lanes = pl.ds(c * LANES, LANES)
        wide[c, :, 0:8, :] = jnp.zeros((6, 8, LANES), jnp.float32)
        wide[c, :, 8 + CELLS_C : 16 + CELLS_C, :] = jnp.zeros((6, 8, LANES), jnp.float32)
        wide[c, 0:3, 8 : 8 + CELLS_C, :] = low_ref[:, :, lanes].astype(jnp.float32)
        wide[c, 3:6, 8 : 8 + CELLS_C, :] = high_ref[:, :, lanes].astype(jnp.float32)

    def lane_tile(c, carry):
        lanes = pl.ds(pl.multiple_of(c * LANES, LANES), LANES)
        for j in range(CELLS_C // 8):
            acc = [acc_in[i, 8 * j : 8 * j + 8, lanes] for i in range(CELLS_R)]
            for b in range(7):
                at = 8 * j + 5 + b
                rows = [wide[c, r, at : at + 8, :] for r in range(6)]
                acc = taps(acc, rows[:3], weight_ref, lanes, b, -3)
                acc = taps(acc, rows[3:], weight_ref, lanes, b, CELLS_R)
            for i in range(CELLS_R):
                acc_ref[i, 8 * j : 8 * j + 8, lanes] = acc[i]
        return carry

    lax.fori_loop(0, 3, lane_tile, 0)


def halo_columns(acc_ref, left_ref, right_ref, weight_ref, edge):
    tall = CELLS_R + 6
    edge[...] = jnp.zeros(edge.shape, jnp.float32)
    for c in range(3):
        lanes = pl.ds(c * LANES, LANES)
        edge[0, c, :, 5:8, :] = left_ref[:, :, lanes].astype(jnp.float32)
        edge[1, c, :, 8:11, :] = right_ref[:, :, lanes].astype(jnp.float32)

    def lane_tile(c, carry):
        lanes = pl.ds(pl.multiple_of(c * LANES, LANES), LANES)
        for side in (0, 1):
            here = slice(8 * side, 8 * side + 8)
            acc = [acc_ref[i, here, lanes] for i in range(CELLS_R)]
            for b in (0, 1, 2) if side == 0 else (4, 5, 6):
                at = 5 + b if side == 0 else b - 3
                rows = [edge[side, c, r, at : at + 8, :] for r in range(tall)]
                acc = taps(acc, rows, weight_ref, lanes, b, -3)
            for i in range(CELLS_R):
                acc_ref[i, here, lanes] = acc[i]
        return carry

    lax.fori_loop(0, 3, lane_tile, 0)


def gelu(x):
    return 0.5 * x * (1.0 + lax.erf(x * (0.5**0.5)))


def block_of(conv_rows, inputs, lines_ref, expand_ref, shrink_ref, normed, hidden):
    gain, norm_bias, shrink_bias, scale = (lines_ref[k : k + 1, :] for k in range(4))
    for i in range(CELLS_R):
        conv = conv_rows(i)
        center = jnp.mean(conv, axis=-1, keepdims=True)
        conv = conv - center
        variance = jnp.mean(conv * conv, axis=-1, keepdims=True)
        normed[i * HALF : (i + 1) * HALF, :] = (
            conv * lax.rsqrt(variance + 1e-06) * gain + norm_bias
        ).astype(jnp.bfloat16)
    for k in range(HID // WIDTH):
        lanes = slice(k * WIDTH, (k + 1) * WIDTH)
        part = jnp.dot(normed[...], expand_ref[:, lanes], preferred_element_type=jnp.float32)
        hidden[:, lanes] = gelu(part + lines_ref[4 + k : 5 + k, :]).astype(jnp.bfloat16)
    shrunk = jnp.dot(hidden[...], shrink_ref[...], preferred_element_type=jnp.float32)
    shrunk = shrunk + shrink_bias
    inputs = inputs.reshape(CELLS_R * HALF, WIDTH).astype(jnp.float32)
    return (inputs + scale * shrunk).astype(jnp.bfloat16)


def keys_of(block, key_ref):
    return jnp.dot(block, key_ref[...], preferred_element_type=jnp.float32).astype(jnp.bfloat16)


def values_of(block, turned_ref):
    return lax.dot_general(
        turned_ref[...], block, (((1,), (1,)), ((), ())), preferred_element_type=jnp.float32
    ).astype(jnp.bfloat16)


def inner_kernel(
    acc_in,
    low_ref,
    high_ref,
    weight_ref,
    x_ref,
    lines_ref,
    expand_ref,
    shrink_ref,
    key_ref,
    turned_ref,
    sides_ref,
    block_ref,
    keys_ref,
    values_ref,
    wide,
    acc_ref,
    normed,
    hidden,
):
    halo_rows(acc_in, low_ref, high_ref, weight_ref, acc_ref, wide)
    sides_ref[:, 0:8, :] = acc_ref[:, 0:8, :]
    sides_ref[:, 8:16, :] = acc_ref[:, CELLS_C - 8 : CELLS_C, :]
    block = block_of(
        lambda i: acc_ref[i, 8 : 8 + HALF, :],
        x_ref[:, 8 : 8 + HALF, :],
        lines_ref,
        expand_ref,
        shrink_ref,
        normed,
        hidden,
    )
    block_ref[...] = block.reshape(CELLS_R, HALF, WIDTH)
    keys_ref[...] = keys_of(block, key_ref)
    values_ref[...] = values_of(block, turned_ref)


def marked(weighted, marks):
    high = marks.astype(jnp.bfloat16).astype(jnp.float32)
    rest = marks - high
    middle = rest.astype(jnp.bfloat16).astype(jnp.float32)
    low = (rest - middle).astype(jnp.bfloat16).astype(jnp.float32)
    marks = high + pltpu.roll(middle, NH, 1) + pltpu.roll(low, 2 * NH, 1)
    return jnp.concatenate([weighted, marks], axis=1).astype(jnp.bfloat16)


def outer_kernel(
    tissue_ref,
    acc_in,
    left_ref,
    right_ref,
    weight_ref,
    x_ref,
    lines_ref,
    expand_ref,
    shrink_ref,
    key_ref,
    turned_ref,
    big_ref,
    block_ref,
    keys_ref,
    values_ref,
    out_ref,
    part_ref,
    acc_ref,
    edge,
    normed,
    hidden,
    sums,
    whole,
    sem,
):
    acc_ref[...] = acc_in[...]
    whole[:, 8 : 8 + HALF, :] = block_ref[...]
    halo_columns(acc_ref, left_ref, right_ref, weight_ref, edge)
    block = block_of(
        lambda i: acc_ref[i],
        jnp.concatenate([x_ref[:, 0:8, :], x_ref[:, CELLS_C - 8 : CELLS_C, :]], axis=1),
        lines_ref,
        expand_ref,
        shrink_ref,
        normed,
        hidden,
    )
    parts = block.reshape(CELLS_R, HALF, WIDTH)
    whole[:, 0:8, :] = parts[:, 0:8, :]
    whole[:, CELLS_C - 8 : CELLS_C, :] = parts[:, 8:16, :]
    copy = pltpu.make_async_copy(whole, out_ref, sem)
    copy.start()
    keys = jnp.concatenate([keys_ref[...], keys_of(block, key_ref)], axis=0)
    values = jnp.concatenate([values_ref[...], values_of(block, turned_ref)], axis=1)
    size = WIDTH // NH
    tiles = ((1, 2), (0, 3))
    live = [[tissue_ref[0, t] > 0 for t in pair] for pair in tiles]
    line = lax.broadcasted_iota(jnp.int32, (NH, LANES), 0)
    tops = jnp.zeros((NH, LANES), jnp.float32)
    totals = jnp.zeros((NH, LANES), jnp.float32)
    for t in range(NH // 2):
        scores = jnp.dot(
            keys, big_ref[:, t * LANES : (t + 1) * LANES], preferred_element_type=jnp.float32
        ) * (size**-0.5 * LOG2E)
        scores = scores.reshape(2, CELLS_R, 2, TILE, LANES)
        scores = [
            [jnp.where(live[h][g], scores[h, :, g], -1e30) for g in range(2)] for h in range(2)
        ]
        top = jnp.maximum(
            jnp.maximum(scores[0][0], scores[0][1]), jnp.maximum(scores[1][0], scores[1][1])
        )
        top = jnp.ceil(jnp.max(jnp.max(top, axis=0), axis=0, keepdims=True))
        weights = [
            [jnp.where(live[h][g], jnp.exp2(scores[h][g] - top), 0.0) for g in range(2)]
            for h in range(2)
        ]
        total = (weights[0][0] + weights[0][1]) + (weights[1][0] + weights[1][1])
        total = jnp.sum(jnp.sum(total, axis=0), axis=0, keepdims=True)
        weights = [jnp.stack(pair, axis=1).reshape(CELLS_R * HALF, LANES) for pair in weights]
        weights = jnp.concatenate(weights, axis=0).astype(jnp.bfloat16)
        pair = jnp.dot(
            values[2 * size * t : 2 * size * (t + 1), :], weights, preferred_element_type=jnp.float32
        )
        sums[2 * size * t : 2 * size * t + size, :] = pair[:size]
        sums[2 * size * t + size : 2 * size * (t + 1), :] = pltpu.roll(pair[size:], NQ, 1)
        top = jnp.broadcast_to(top, (NH, LANES))
        total = jnp.broadcast_to(total, (NH, LANES))
        tops = jnp.where(line == 2 * t, top, tops)
        tops = jnp.where(line == 2 * t + 1, pltpu.roll(top, NQ, 1), tops)
        totals = jnp.where(line == 2 * t, total, totals)
        totals = jnp.where(line == 2 * t + 1, pltpu.roll(total, NQ, 1), totals)
    sums[WIDTH:, :] = jnp.zeros((LANES, LANES), jnp.float32)
    sums[WIDTH : WIDTH + NH, :] = tops
    sums[WIDTH + 3 * NH : WIDTH + 4 * NH, :] = totals
    part = sums[...].T
    part_ref[...] = jnp.broadcast_to(
        marked(part[:NQ, :WIDTH], part[:NQ, WIDTH:])[None], part_ref.shape
    )
    copy.wait()


def spread_matrix(first, copies):
    lane = lax.broadcasted_iota(jnp.int32, (LANES, WIDTH), 0) - first
    head = lax.broadcasted_iota(jnp.int32, (LANES, WIDTH), 1) // (WIDTH // NH)
    inside = (lane >= 0) & (lane < copies * NH)
    return jnp.where(inside & (lane % NH == head), 1.0, 0.0).astype(jnp.bfloat16)


def combined(parts):
    n, q = parts.shape[:2]
    parts = parts.astype(jnp.float32)
    marks = parts[:, :, WIDTH:].reshape(n * q, LANES)
    marks = marks + pltpu.roll(marks, LANES - NH, 1) + pltpu.roll(marks, LANES - 2 * NH, 1)
    top = jnp.max(marks.reshape(n, q, LANES), axis=0)
    factor = jnp.exp2(marks.reshape(n, q, LANES) - top).reshape(n * q, LANES)
    factor = factor.astype(jnp.bfloat16)
    spread = jnp.dot(factor, spread_matrix(0, 1), preferred_element_type=jnp.float32)
    weighted = jnp.sum(parts[:, :, :WIDTH] * spread.reshape(n, q, WIDTH), axis=0)
    total = marks * pltpu.roll(factor.astype(jnp.float32), 3 * NH, 1)
    total = jnp.sum(total.reshape(n, q, LANES), axis=0)
    lane = lax.broadcasted_iota(jnp.int32, (q, LANES), 1)
    inside = (lane >= 3 * NH) & (lane < 4 * NH)
    return weighted, jnp.where(lane < NH, top, 0.0), jnp.where(inside, total, 1.0), inside


def merge_kernel(parts_ref, out_ref):
    weighted, top, total, inside = combined(parts_ref[...])
    part = marked(weighted, top + jnp.where(inside, total, 0.0))
    out_ref[...] = jnp.broadcast_to(part[None], out_ref.shape)


def pool_kernel(parts_ref, class_ref, label_ref, out_ref, loss_ref):
    weighted, _, total, inside = combined(parts_ref[...].reshape(2, NQ, WIDTH + LANES))
    marks = marked(weighted, jnp.where(inside, 1.0 / total, 0.0))[:, WIDTH:]
    inverse = jnp.dot(marks, spread_matrix(3 * NH, 3), preferred_element_type=jnp.float32)
    pooled = weighted * inverse
    out_ref[...] = pooled
    lines = jnp.sum(pooled.reshape(NQ // 8, 8, WIDTH), axis=0)
    logits = lax.dot_general(
        lines,
        class_ref[...],
        (((1,), (1,)), ((), ())),
        precision=lax.Precision.HIGHEST,
        preferred_element_type=jnp.float32,
    )
    logits = jnp.sum(logits, axis=0, keepdims=True)
    label = label_ref[...].reshape(logits.shape).astype(jnp.float32)
    soft = jnp.maximum(logits, 0.0) + jnp.log1p(jnp.exp(-jnp.abs(logits)))
    loss_ref[0] = jnp.sum(soft - label * logits)


def everyone(part, groups):
    return lax.all_to_all(part, ("row", "col"), 0, 0, axis_index_groups=groups, tiled=True)


def call(kernel, out_shape, name, *args, **more):
    return pl.pallas_call(kernel, out_shape=out_shape, name=name, **more, **params())(*args)


def merged(part, class_weight, slide_label):
    chunk = (16, NQ // 8, WIDTH + LANES)
    same = jax.ShapeDtypeStruct(chunk, jnp.bfloat16)
    parts = everyone(part.reshape(chunk), FIRST)
    parts = everyone(call(merge_kernel, same, "merge_first", parts), SECOND)
    parts = everyone(call(merge_kernel, same, "merge_second", parts), THIRD)
    return call(
        pool_kernel,
        (jax.ShapeDtypeStruct((NQ, WIDTH), jnp.float32), jax.ShapeDtypeStruct((1,), jnp.float32)),
        "pool",
        parts,
        class_weight.T,
        slide_label,
        out_specs=(pl.BlockSpec(memory_space=pltpu.VMEM), pl.BlockSpec(memory_space=pltpu.SMEM)),
    )


def vmem(*shape):
    return pltpu.VMEM(shape, jnp.float32)


def params(flops=1000000):
    return dict(
        compiler_params=pltpu.CompilerParams(vmem_limit_bytes=24 * 1024 * 1024),
        cost_estimate=pl.CostEstimate(flops=flops, bytes_accessed=1000000, transcendentals=0),
    )


def exchanged(first, last, axis):
    count, odd = lax.axis_size(axis), lax.axis_index(axis) % 2 == 1
    inner = [(i, i ^ 1) for i in range(count)]
    outer = [(i, i + 1 if i % 2 else i - 1) for i in range(1, count - 1)]
    near = lax.ppermute(jnp.where(odd, first, last), axis, inner)
    far = lax.ppermute(jnp.where(odd, last, first), axis, outer)
    return jnp.where(odd, near, far), jnp.where(odd, far, near)


def per_device(
    features,
    depth_weight,
    depth_bias,
    norm_gain,
    norm_bias,
    expand_weight,
    expand_bias,
    shrink_weight,
    shrink_bias,
    layer_scale,
    key_weight,
    value_weight,
    queries,
    class_weight,
    tissue,
    slide_label,
):
    rows, cols, width = features.shape
    f32, bf16 = jnp.float32, jnp.bfloat16
    hbm, whole = pl.BlockSpec(memory_space=pltpu.HBM), pl.BlockSpec(memory_space=pltpu.VMEM)
    shaped = jax.ShapeDtypeStruct
    low, high = exchanged(features[:3], features[-3:], "row")
    acc, first, last, cells, taps_, expand, shrink, key, turned, big, lines = call(
        own_kernel,
        (
            shaped((rows, cols, width), f32),
            shaped((rows, 3, width), bf16),
            shaped((rows, 3, width), bf16),
            shaped(features.shape, bf16),
            shaped(depth_weight.shape, f32),
            shaped(expand_weight.shape, bf16),
            shaped(shrink_weight.shape, bf16),
            shaped(key_weight.shape, bf16),
            shaped(value_weight.shape, bf16),
            shaped((width, NH * NQ), bf16),
            shaped((16, width), f32),
        ),
        "own_cells",
        *(
            pltpu.with_memory_space_constraint(array, pltpu.HBM)
            for array in (
                features,
                depth_weight,
                expand_weight,
                shrink_weight,
                key_weight,
                value_weight,
                queries,
                depth_bias,
                norm_gain,
                norm_bias,
                shrink_bias,
                layer_scale,
                expand_bias,
            )
        ),
        in_specs=[hbm] * 13,
        out_specs=(whole,) * 11,
        scratch_shapes=[
            vmem(3, rows, cols + 16, LANES),
            pltpu.VMEM(value_weight.shape, bf16),
            pltpu.VMEM(queries.shape, bf16),
            *(vmem(width) for _ in range(5)),
            vmem(HID),
            pltpu.SemaphoreType.DMA((13,)),
        ],
    )
    left, right = exchanged(
        jnp.concatenate([low[:, :3], first, high[:, :3]], axis=0),
        jnp.concatenate([low[:, -3:], last, high[:, -3:]], axis=0),
        "col",
    )
    count = rows * HALF
    work = [pltpu.VMEM((count, width), bf16), pltpu.VMEM((count, HID), bf16)]
    sides, inner, keys, values = call(
        inner_kernel,
        (
            shaped((rows, HALF, width), f32),
            shaped((rows, HALF, width), bf16),
            shaped((count, width), bf16),
            shaped((width, count), bf16),
        ),
        "inner_cells",
        acc,
        low,
        high,
        taps_,
        cells,
        lines,
        expand,
        shrink,
        key,
        turned,
        scratch_shapes=[vmem(3, 6, cols + 16, LANES), vmem(rows, cols, width), *work],
    )
    block_out, part = call(
        outer_kernel,
        (shaped((rows, cols, width), bf16), shaped((2, NQ, width + LANES), bf16)),
        "outer_cells",
        tissue,
        sides,
        left,
        right,
        taps_,
        cells,
        lines,
        expand,
        shrink,
        key,
        turned,
        big,
        inner,
        keys,
        values,
        in_specs=[pl.BlockSpec(memory_space=pltpu.SMEM)] + [whole] * 14,
        out_specs=(hbm, whole),
        scratch_shapes=[
            vmem(rows, HALF, width),
            vmem(2, 3, rows + 6, 16, LANES),
            *work,
            vmem(width + LANES, LANES),
            pltpu.VMEM((rows, cols, width), bf16),
            pltpu.SemaphoreType.DMA,
        ],
    )
    pooled, slide_loss = merged(part, class_weight, slide_label)
    return (block_out, pooled, slide_loss)


def solution(mesh):
    placed = (P("row", "col", None),) + (P(),) * 13 + (P("row", "col"), P())
    return jax.shard_map(
        per_device,
        mesh=mesh,
        in_specs=placed,
        out_specs=(P("row", "col", None), P(), P()),
        check_vma=False,
    )
```

```python
import jax
import jax.numpy as jnp
from jax import lax
from jax.experimental import pallas as pl
from jax.experimental.pallas import tpu as pltpu
from jax.sharding import PartitionSpec as P

NH = 8
NQ = 64
TILE = 8
LOG2E = 1.4426950408889634


def device(z, near, y):
    return (z * 8 + near) * 8 + y


EIGHT, FOUR, TWO = range(8), range(4), range(2)
FIRST = [[device(2 * z + k, n, y) for k in TWO for n in EIGHT] for z in FOUR for y in EIGHT]
SECOND = [
    [device(2 * z + k, n, 2 * y + m) for z in FOUR for y in FOUR]
    for k in TWO
    for n in EIGHT
    for m in TWO
]
THIRD = [[device(z, n, 2 * y + m) for m in TWO for n in EIGHT] for z in EIGHT for y in FOUR]


WIDTH = 384
LANES = 128
CELLS_R = 8
CELLS_C = 32
HID = 1536
HALF = 16


def taps(acc, rows, weight_ref, lanes, b, first):
    for a in range(7):
        weight = weight_ref[a, b : b + 1, lanes]
        for i in range(CELLS_R):
            at = i + a - 3 - first
            if 0 <= at < len(rows):
                acc[i] = acc[i] + rows[at] * weight
    return acc


def fetch_kernel(
    x_hbm, weight_hbm, bias_hbm, x_ref, weight_ref, bias_ref, inner_ref, outer_ref, first_ref, last_ref, sems
):
    pairs = ((x_hbm, x_ref), (weight_hbm, weight_ref), (bias_hbm, bias_ref))
    copies = [pltpu.make_async_copy(s, d, sems.at[k]) for k, (s, d) in enumerate(pairs)]
    for copy in copies:
        copy.start()
    copies[0].wait()
    odd = lax.axis_index("row") % 2
    inner_ref[...] = x_ref[pl.ds((1 - odd) * (CELLS_R - 3), 3)]
    outer_ref[...] = x_ref[pl.ds(odd * (CELLS_R - 3), 3)]
    first_ref[...] = x_ref[:, 0:3, :]
    last_ref[...] = x_ref[:, CELLS_C - 3 : CELLS_C, :]
    for copy in copies[1:]:
        copy.wait()


def own_kernel(
    x_ref,
    weight_ref,
    bias_ref,
    expand_hbm,
    key_hbm,
    value_hbm,
    query_hbm,
    gain_hbm,
    norm_bias_hbm,
    shrink_bias_hbm,
    scale_hbm,
    expand_bias_hbm,
    acc_ref,
    expand_ref,
    key_ref,
    turned_ref,
    query_ref,
    rows_ref,
    wide,
    value_ref,
    gain_ref,
    norm_bias_ref,
    shrink_bias_ref,
    scale_ref,
    expand_bias_ref,
    sems,
):
    pairs = (
        (gain_hbm, gain_ref),
        (norm_bias_hbm, norm_bias_ref),
        (shrink_bias_hbm, shrink_bias_ref),
        (scale_hbm, scale_ref),
        (expand_bias_hbm, expand_bias_ref),
        (query_hbm, query_ref),
        (value_hbm, value_ref),
        (key_hbm, key_ref),
        *(
            (expand_hbm.at[k : k + LANES], expand_ref.at[k : k + LANES])
            for k in range(0, WIDTH, LANES)
        ),
    )
    copies = [pltpu.make_async_copy(s, d, sems.at[k]) for k, (s, d) in enumerate(pairs)]
    for copy in copies:
        copy.start()
    rows_ref[8:9, :] = bias_ref[...].reshape(1, WIDTH)
    for c in range(3):
        lanes = pl.ds(c * LANES, LANES)
        wide[c, :, 0:8, :] = jnp.zeros((CELLS_R, 8, LANES), jnp.float32)
        wide[c, :, 8 + CELLS_C : 16 + CELLS_C, :] = jnp.zeros((CELLS_R, 8, LANES), jnp.float32)
        wide[c, :, 8 : 8 + CELLS_C, :] = x_ref[:, :, lanes].astype(jnp.float32)

    def lane_tile(c, carry):
        lanes = pl.ds(pl.multiple_of(c * LANES, LANES), LANES)
        bias = jnp.broadcast_to(rows_ref[8:9, lanes], (8, LANES))
        for j in range(CELLS_C // 8):
            acc = [bias] * CELLS_R
            for b in range(7):
                at = 8 * j + 5 + b
                rows = [wide[c, r, at : at + 8, :] for r in range(CELLS_R)]
                acc = taps(acc, rows, weight_ref, lanes, b, 0)
            for i in range(CELLS_R):
                acc_ref[i, 8 * j : 8 * j + 8, lanes] = acc[i]
        return carry

    lax.fori_loop(0, 3, lane_tile, 0)
    for copy in copies:
        copy.wait()
    turned_ref[...] = value_ref[...].astype(jnp.float32).T.astype(jnp.bfloat16)
    for row, ref in enumerate((gain_ref, norm_bias_ref, shrink_bias_ref, scale_ref)):
        rows_ref[row : row + 1, :] = ref[...].reshape(1, WIDTH)
    for k in range(HID // WIDTH):
        rows_ref[4 + k : 5 + k, :] = expand_bias_ref[k * WIDTH : (k + 1) * WIDTH].reshape(1, WIDTH)


def halo_rows(acc_in, low_ref, high_ref, weight_ref, acc_ref, wide):
    for c in range(3):
        lanes = pl.ds(c * LANES, LANES)
        wide[c, :, 0:8, :] = jnp.zeros((6, 8, LANES), jnp.float32)
        wide[c, :, 8 + CELLS_C : 16 + CELLS_C, :] = jnp.zeros((6, 8, LANES), jnp.float32)
        wide[c, 0:3, 8 : 8 + CELLS_C, :] = low_ref[:, :, lanes].astype(jnp.float32)
        wide[c, 3:6, 8 : 8 + CELLS_C, :] = high_ref[:, :, lanes].astype(jnp.float32)

    def lane_tile(c, carry):
        lanes = pl.ds(pl.multiple_of(c * LANES, LANES), LANES)
        for j in range(CELLS_C // 8):
            acc = [acc_in[i, 8 * j : 8 * j + 8, lanes] for i in range(CELLS_R)]
            for b in range(7):
                at = 8 * j + 5 + b
                rows = [wide[c, r, at : at + 8, :] for r in range(6)]
                acc = taps(acc, rows[:3], weight_ref, lanes, b, -3)
                acc = taps(acc, rows[3:], weight_ref, lanes, b, CELLS_R)
            for i in range(CELLS_R):
                acc_ref[i, 8 * j : 8 * j + 8, lanes] = acc[i]
        return carry

    lax.fori_loop(0, 3, lane_tile, 0)


def halo_columns(acc_ref, left_ref, right_ref, weight_ref, edge):
    tall = CELLS_R + 6
    edge[...] = jnp.zeros(edge.shape, jnp.float32)
    for c in range(3):
        lanes = pl.ds(c * LANES, LANES)
        edge[0, c, :, 5:8, :] = left_ref[:, :, lanes].astype(jnp.float32)
        edge[1, c, :, 8:11, :] = right_ref[:, :, lanes].astype(jnp.float32)

    def lane_tile(c, carry):
        lanes = pl.ds(pl.multiple_of(c * LANES, LANES), LANES)
        for side in (0, 1):
            here = slice(8 * side, 8 * side + 8)
            acc = [acc_ref[i, here, lanes] for i in range(CELLS_R)]
            for b in (0, 1, 2) if side == 0 else (4, 5, 6):
                at = 5 + b if side == 0 else b - 3
                rows = [edge[side, c, r, at : at + 8, :] for r in range(tall)]
                acc = taps(acc, rows, weight_ref, lanes, b, -3)
            for i in range(CELLS_R):
                acc_ref[i, here, lanes] = acc[i]
        return carry

    lax.fori_loop(0, 3, lane_tile, 0)


def gelu(x):
    return 0.5 * x * (1.0 + lax.erf(x * (0.5**0.5)))


def block_of(conv_rows, inputs, lines_ref, expand_ref, shrink_ref, normed, hidden, copies=()):
    gain, norm_bias, shrink_bias, scale = (lines_ref[k : k + 1, :] for k in range(4))
    for i in range(CELLS_R):
        conv = conv_rows(i)
        center = jnp.mean(conv, axis=-1, keepdims=True)
        conv = conv - center
        variance = jnp.mean(conv * conv, axis=-1, keepdims=True)
        normed[i * HALF : (i + 1) * HALF, :] = (
            conv * lax.rsqrt(variance + 1e-06) * gain + norm_bias
        ).astype(jnp.bfloat16)
    for k in range(HID // WIDTH):
        lanes = slice(k * WIDTH, (k + 1) * WIDTH)
        part = jnp.dot(normed[...], expand_ref[:, lanes], preferred_element_type=jnp.float32)
        hidden[:, lanes] = gelu(part + lines_ref[4 + k : 5 + k, :]).astype(jnp.bfloat16)
    for copy in copies:
        copy.wait()
    shrunk = jnp.dot(hidden[...], shrink_ref[...], preferred_element_type=jnp.float32)
    shrunk = shrunk + shrink_bias
    inputs = inputs.reshape(CELLS_R * HALF, WIDTH).astype(jnp.float32)
    return (inputs + scale * shrunk).astype(jnp.bfloat16)


def keys_of(block, key_ref):
    return jnp.dot(block, key_ref[...], preferred_element_type=jnp.float32).astype(jnp.bfloat16)


def values_of(block, turned_ref):
    return lax.dot_general(
        turned_ref[...], block, (((1,), (1,)), ((), ())), preferred_element_type=jnp.float32
    ).astype(jnp.bfloat16)


def inner_kernel(
    acc_in,
    low_ref,
    high_ref,
    weight_ref,
    x_ref,
    lines_ref,
    expand_ref,
    shrink_hbm,
    key_ref,
    turned_ref,
    query_ref,
    sides_ref,
    block_ref,
    keys_ref,
    values_ref,
    shrink_ref,
    big_ref,
    wide,
    acc_ref,
    normed,
    hidden,
    sems,
):
    copies = [
        pltpu.make_async_copy(
            shrink_hbm.at[k * WIDTH : (k + 1) * WIDTH],
            shrink_ref.at[k * WIDTH : (k + 1) * WIDTH],
            sems.at[k],
        )
        for k in range(HID // WIDTH)
    ]
    for copy in copies:
        copy.start()
    halo_rows(acc_in, low_ref, high_ref, weight_ref, acc_ref, wide)
    query = query_ref[...].astype(jnp.float32)
    query = jnp.concatenate([query, query], axis=0).T
    head = lax.broadcasted_iota(jnp.int32, (WIDTH, LANES), 0) // (WIDTH // NH)
    half = lax.broadcasted_iota(jnp.int32, (WIDTH, LANES), 1) // NQ
    for t in range(NH // 2):
        big_ref[:, t * LANES : (t + 1) * LANES] = jnp.where(
            head == 2 * t + half, query, 0.0
        ).astype(jnp.bfloat16)
    sides_ref[:, 0:8, :] = acc_ref[:, 0:8, :]
    sides_ref[:, 8:16, :] = acc_ref[:, CELLS_C - 8 : CELLS_C, :]
    block = block_of(
        lambda i: acc_ref[i, 8 : 8 + HALF, :],
        x_ref[:, 8 : 8 + HALF, :],
        lines_ref,
        expand_ref,
        shrink_ref,
        normed,
        hidden,
        copies,
    )
    block_ref[...] = block.reshape(CELLS_R, HALF, WIDTH)
    keys_ref[...] = keys_of(block, key_ref)
    values_ref[...] = values_of(block, turned_ref)


def marked(weighted, marks):
    high = marks.astype(jnp.bfloat16).astype(jnp.float32)
    rest = marks - high
    middle = rest.astype(jnp.bfloat16).astype(jnp.float32)
    low = (rest - middle).astype(jnp.bfloat16).astype(jnp.float32)
    marks = high + pltpu.roll(middle, NH, 1) + pltpu.roll(low, 2 * NH, 1)
    return jnp.concatenate([weighted, marks], axis=1).astype(jnp.bfloat16)


def outer_kernel(
    tissue_ref,
    acc_in,
    left_ref,
    right_ref,
    weight_ref,
    x_ref,
    lines_ref,
    expand_ref,
    shrink_ref,
    key_ref,
    turned_ref,
    big_ref,
    block_ref,
    keys_ref,
    values_ref,
    out_ref,
    part_ref,
    acc_ref,
    edge,
    normed,
    hidden,
    sums,
    whole,
    sem,
):
    acc_ref[...] = acc_in[...]
    whole[:, 8 : 8 + HALF, :] = block_ref[...]
    halo_columns(acc_ref, left_ref, right_ref, weight_ref, edge)
    block = block_of(
        lambda i: acc_ref[i],
        jnp.concatenate([x_ref[:, 0:8, :], x_ref[:, CELLS_C - 8 : CELLS_C, :]], axis=1),
        lines_ref,
        expand_ref,
        shrink_ref,
        normed,
        hidden,
    )
    parts = block.reshape(CELLS_R, HALF, WIDTH)
    whole[:, 0:8, :] = parts[:, 0:8, :]
    whole[:, CELLS_C - 8 : CELLS_C, :] = parts[:, 8:16, :]
    copy = pltpu.make_async_copy(whole, out_ref, sem)
    copy.start()
    keys = jnp.concatenate([keys_ref[...], keys_of(block, key_ref)], axis=0)
    values = jnp.concatenate([values_ref[...], values_of(block, turned_ref)], axis=1)
    size = WIDTH // NH
    tiles = ((1, 2), (0, 3))
    live = [[tissue_ref[0, t] > 0 for t in pair] for pair in tiles]
    line = lax.broadcasted_iota(jnp.int32, (NH, LANES), 0)
    tops = jnp.zeros((NH, LANES), jnp.float32)
    totals = jnp.zeros((NH, LANES), jnp.float32)
    for t in range(NH // 2):
        scores = jnp.dot(
            keys, big_ref[:, t * LANES : (t + 1) * LANES], preferred_element_type=jnp.float32
        ) * (size**-0.5 * LOG2E)
        scores = scores.reshape(2, CELLS_R, 2, TILE, LANES)
        scores = [
            [jnp.where(live[h][g], scores[h, :, g], -1e30) for g in range(2)] for h in range(2)
        ]
        top = jnp.maximum(
            jnp.maximum(scores[0][0], scores[0][1]), jnp.maximum(scores[1][0], scores[1][1])
        )
        top = jnp.ceil(jnp.max(jnp.max(top, axis=0), axis=0, keepdims=True))
        weights = [
            [jnp.where(live[h][g], jnp.exp2(scores[h][g] - top), 0.0) for g in range(2)]
            for h in range(2)
        ]
        total = (weights[0][0] + weights[0][1]) + (weights[1][0] + weights[1][1])
        total = jnp.sum(jnp.sum(total, axis=0), axis=0, keepdims=True)
        weights = [jnp.stack(pair, axis=1).reshape(CELLS_R * HALF, LANES) for pair in weights]
        weights = jnp.concatenate(weights, axis=0).astype(jnp.bfloat16)
        pair = jnp.dot(
            values[2 * size * t : 2 * size * (t + 1), :], weights, preferred_element_type=jnp.float32
        )
        sums[2 * size * t : 2 * size * t + size, :] = pair[:size]
        sums[2 * size * t + size : 2 * size * (t + 1), :] = pltpu.roll(pair[size:], NQ, 1)
        top = jnp.broadcast_to(top, (NH, LANES))
        total = jnp.broadcast_to(total, (NH, LANES))
        tops = jnp.where(line == 2 * t, top, tops)
        tops = jnp.where(line == 2 * t + 1, pltpu.roll(top, NQ, 1), tops)
        totals = jnp.where(line == 2 * t, total, totals)
        totals = jnp.where(line == 2 * t + 1, pltpu.roll(total, NQ, 1), totals)
    sums[WIDTH:, :] = jnp.zeros((LANES, LANES), jnp.float32)
    sums[WIDTH : WIDTH + NH, :] = tops
    sums[WIDTH + 3 * NH : WIDTH + 4 * NH, :] = totals
    part = sums[...].T
    part_ref[...] = jnp.broadcast_to(
        marked(part[:NQ, :WIDTH], part[:NQ, WIDTH:])[None], part_ref.shape
    )
    copy.wait()


def spread_matrix(first, copies):
    lane = lax.broadcasted_iota(jnp.int32, (LANES, WIDTH), 0) - first
    head = lax.broadcasted_iota(jnp.int32, (LANES, WIDTH), 1) // (WIDTH // NH)
    inside = (lane >= 0) & (lane < copies * NH)
    return jnp.where(inside & (lane % NH == head), 1.0, 0.0).astype(jnp.bfloat16)


def combined(parts):
    n, q = parts.shape[:2]
    parts = parts.astype(jnp.float32)
    marks = parts[:, :, WIDTH:].reshape(n * q, LANES)
    marks = marks + pltpu.roll(marks, LANES - NH, 1) + pltpu.roll(marks, LANES - 2 * NH, 1)
    top = jnp.max(marks.reshape(n, q, LANES), axis=0)
    factor = jnp.exp2(marks.reshape(n, q, LANES) - top).reshape(n * q, LANES)
    factor = factor.astype(jnp.bfloat16)
    spread = jnp.dot(factor, spread_matrix(0, 1), preferred_element_type=jnp.float32)
    weighted = jnp.sum(parts[:, :, :WIDTH] * spread.reshape(n, q, WIDTH), axis=0)
    total = marks * pltpu.roll(factor.astype(jnp.float32), 3 * NH, 1)
    total = jnp.sum(total.reshape(n, q, LANES), axis=0)
    lane = lax.broadcasted_iota(jnp.int32, (q, LANES), 1)
    inside = (lane >= 3 * NH) & (lane < 4 * NH)
    return weighted, jnp.where(lane < NH, top, 0.0), jnp.where(inside, total, 1.0), inside


def merge_kernel(parts_ref, out_ref):
    weighted, top, total, inside = combined(parts_ref[...])
    part = marked(weighted, top + jnp.where(inside, total, 0.0))
    out_ref[...] = jnp.broadcast_to(part[None], out_ref.shape)


def pool_kernel(parts_ref, class_ref, label_ref, out_ref, loss_ref):
    weighted, _, total, inside = combined(parts_ref[...].reshape(2, NQ, WIDTH + LANES))
    marks = marked(weighted, jnp.where(inside, 1.0 / total, 0.0))[:, WIDTH:]
    inverse = jnp.dot(marks, spread_matrix(3 * NH, 3), preferred_element_type=jnp.float32)
    pooled = weighted * inverse
    out_ref[...] = pooled
    lines = jnp.sum(pooled.reshape(NQ // 8, 8, WIDTH), axis=0)
    logits = lax.dot_general(
        lines,
        class_ref[...],
        (((1,), (1,)), ((), ())),
        precision=lax.Precision.HIGHEST,
        preferred_element_type=jnp.float32,
    )
    logits = jnp.sum(logits, axis=0, keepdims=True)
    label = label_ref[...].reshape(logits.shape).astype(jnp.float32)
    soft = jnp.maximum(logits, 0.0) + jnp.log1p(jnp.exp(-jnp.abs(logits)))
    loss_ref[0] = jnp.sum(soft - label * logits)


def everyone(part, groups):
    return lax.all_to_all(part, ("row", "col"), 0, 0, axis_index_groups=groups, tiled=True)


def call(kernel, out_shape, name, *args, **more):
    return pl.pallas_call(kernel, out_shape=out_shape, name=name, **more, **params())(*args)


def merged(part, class_weight, slide_label):
    chunk = (16, NQ // 8, WIDTH + LANES)
    same = jax.ShapeDtypeStruct(chunk, jnp.bfloat16)
    parts = everyone(part.reshape(chunk), FIRST)
    parts = everyone(call(merge_kernel, same, "merge_first", parts), SECOND)
    parts = everyone(call(merge_kernel, same, "merge_second", parts), THIRD)
    return call(
        pool_kernel,
        (jax.ShapeDtypeStruct((NQ, WIDTH), jnp.float32), jax.ShapeDtypeStruct((1,), jnp.float32)),
        "pool",
        parts,
        class_weight.T,
        slide_label,
        out_specs=(pl.BlockSpec(memory_space=pltpu.VMEM), pl.BlockSpec(memory_space=pltpu.SMEM)),
    )


def vmem(*shape):
    return pltpu.VMEM(shape, jnp.float32)


def params(flops=1000000):
    return dict(
        compiler_params=pltpu.CompilerParams(vmem_limit_bytes=24 * 1024 * 1024),
        cost_estimate=pl.CostEstimate(flops=flops, bytes_accessed=1000000, transcendentals=0),
    )


def swapped(near, far, axis):
    count, odd = lax.axis_size(axis), lax.axis_index(axis) % 2 == 1
    inner = [(i, i ^ 1) for i in range(count)]
    outer = [(i, i + 1 if i % 2 else i - 1) for i in range(1, count - 1)]
    near, far = lax.ppermute(near, axis, inner), lax.ppermute(far, axis, outer)
    return jnp.where(odd, near, far), jnp.where(odd, far, near)


def exchanged(first, last, axis):
    odd = lax.axis_index(axis) % 2 == 1
    return swapped(jnp.where(odd, first, last), jnp.where(odd, last, first), axis)


def per_device(
    features,
    depth_weight,
    depth_bias,
    norm_gain,
    norm_bias,
    expand_weight,
    expand_bias,
    shrink_weight,
    shrink_bias,
    layer_scale,
    key_weight,
    value_weight,
    queries,
    class_weight,
    tissue,
    slide_label,
):
    rows, cols, width = features.shape
    f32, bf16 = jnp.float32, jnp.bfloat16
    hbm, whole = pl.BlockSpec(memory_space=pltpu.HBM), pl.BlockSpec(memory_space=pltpu.VMEM)
    shaped = jax.ShapeDtypeStruct
    cells, taps_, bias, near, far, first, last = call(
        fetch_kernel,
        (
            shaped(features.shape, bf16),
            shaped(depth_weight.shape, f32),
            shaped(depth_bias.shape, f32),
            *[shaped((3, cols, width), bf16)] * 2,
            *[shaped((rows, 3, width), bf16)] * 2,
        ),
        "fetch_cells",
        *(
            pltpu.with_memory_space_constraint(array, pltpu.HBM)
            for array in (features, depth_weight, depth_bias)
        ),
        in_specs=[hbm] * 3,
        out_specs=(whole,) * 7,
        scratch_shapes=[pltpu.SemaphoreType.DMA((3,))],
    )
    low, high = swapped(near, far, "row")
    acc, expand, key, turned, query, lines = call(
        own_kernel,
        (
            shaped((rows, cols, width), f32),
            shaped(expand_weight.shape, bf16),
            shaped(key_weight.shape, bf16),
            shaped(value_weight.shape, bf16),
            shaped(queries.shape, bf16),
            shaped((16, width), f32),
        ),
        "own_cells",
        cells,
        taps_,
        bias,
        *(
            pltpu.with_memory_space_constraint(array, pltpu.HBM)
            for array in (
                expand_weight,
                key_weight,
                value_weight,
                queries,
                norm_gain,
                norm_bias,
                shrink_bias,
                layer_scale,
                expand_bias,
            )
        ),
        in_specs=[whole] * 3 + [hbm] * 9,
        out_specs=(whole,) * 6,
        scratch_shapes=[
            vmem(3, rows, cols + 16, LANES),
            pltpu.VMEM(value_weight.shape, bf16),
            *(vmem(width) for _ in range(4)),
            vmem(HID),
            pltpu.SemaphoreType.DMA((11,)),
        ],
    )
    first, last, acc = lax.optimization_barrier((first, last, acc))
    left, right = exchanged(
        jnp.concatenate([low[:, :3], first, high[:, :3]], axis=0),
        jnp.concatenate([low[:, -3:], last, high[:, -3:]], axis=0),
        "col",
    )
    count = rows * HALF
    work = [pltpu.VMEM((count, width), bf16), pltpu.VMEM((count, HID), bf16)]
    sides, inner, keys, values, shrink, big = call(
        inner_kernel,
        (
            shaped((rows, HALF, width), f32),
            shaped((rows, HALF, width), bf16),
            shaped((count, width), bf16),
            shaped((width, count), bf16),
            shaped(shrink_weight.shape, bf16),
            shaped((width, NH * NQ), bf16),
        ),
        "inner_cells",
        acc,
        low,
        high,
        taps_,
        cells,
        lines,
        expand,
        pltpu.with_memory_space_constraint(shrink_weight, pltpu.HBM),
        key,
        turned,
        query,
        in_specs=[whole] * 7 + [hbm] + [whole] * 3,
        out_specs=(whole,) * 6,
        scratch_shapes=[
            vmem(3, 6, cols + 16, LANES),
            vmem(rows, cols, width),
            *work,
            pltpu.SemaphoreType.DMA((HID // width,)),
        ],
    )
    block_out, part = call(
        outer_kernel,
        (shaped((rows, cols, width), bf16), shaped((2, NQ, width + LANES), bf16)),
        "outer_cells",
        tissue,
        sides,
        left,
        right,
        taps_,
        cells,
        lines,
        expand,
        shrink,
        key,
        turned,
        big,
        inner,
        keys,
        values,
        in_specs=[pl.BlockSpec(memory_space=pltpu.SMEM)] + [whole] * 14,
        out_specs=(hbm, whole),
        scratch_shapes=[
            vmem(rows, HALF, width),
            vmem(2, 3, rows + 6, 16, LANES),
            *work,
            vmem(width + LANES, LANES),
            pltpu.VMEM((rows, cols, width), bf16),
            pltpu.SemaphoreType.DMA,
        ],
    )
    pooled, slide_loss = merged(part, class_weight, slide_label)
    return (block_out, pooled, slide_loss)


def solution(mesh):
    placed = (P("row", "col", None),) + (P(),) * 13 + (P("row", "col"), P())
    return jax.shard_map(
        per_device,
        mesh=mesh,
        in_specs=placed,
        out_specs=(P("row", "col", None), P(), P()),
        check_vma=False,
    )
```

```python
import jax
import jax.numpy as jnp
from jax import lax
from jax.experimental import pallas as pl
from jax.experimental.pallas import tpu as pltpu
from jax.sharding import PartitionSpec as P

NH = 8
NQ = 64
TILE = 8
LOG2E = 1.4426950408889634


def device(z, near, y):
    return (z * 8 + near) * 8 + y


EIGHT, FOUR, TWO = range(8), range(4), range(2)
SHARES = [[device(2 * z + k, n, y) for k in TWO for n in EIGHT] for z in FOUR for y in EIGHT]
REST = [[device(2 * z + k, n, y) for z in FOUR for y in EIGHT] for k in TWO for n in EIGHT]
WIDTH = 384
LANES = 128
CELLS_R = 8
CELLS_C = 32
HID = 1536
HALF = 16
SHARE = 192
MARK = SHARE - LANES


def taps(acc, rows, weight_ref, lanes, b, first):
    for a in range(7):
        weight = weight_ref[a, b : b + 1, lanes]
        for i in range(CELLS_R):
            at = i + a - 3 - first
            if 0 <= at < len(rows):
                acc[i] = acc[i] + rows[at] * weight
    return acc


def fetch_kernel(
    x_hbm, weight_hbm, bias_hbm, x_ref, weight_ref, bias_ref, inner_ref, outer_ref, first_ref, last_ref, sems
):
    pairs = ((x_hbm, x_ref), (weight_hbm, weight_ref), (bias_hbm, bias_ref))
    copies = [pltpu.make_async_copy(s, d, sems.at[k]) for k, (s, d) in enumerate(pairs)]
    for copy in copies:
        copy.start()
    copies[0].wait()
    odd = lax.axis_index("row") % 2
    inner_ref[...] = x_ref[pl.ds((1 - odd) * (CELLS_R - 3), 3)]
    outer_ref[...] = x_ref[pl.ds(odd * (CELLS_R - 3), 3)]
    first_ref[...] = x_ref[:, 0:3, :]
    last_ref[...] = x_ref[:, CELLS_C - 3 : CELLS_C, :]
    for copy in copies[1:]:
        copy.wait()


def own_kernel(
    x_ref,
    weight_ref,
    bias_ref,
    expand_hbm,
    key_hbm,
    value_hbm,
    query_hbm,
    gain_hbm,
    norm_bias_hbm,
    shrink_bias_hbm,
    scale_hbm,
    expand_bias_hbm,
    acc_ref,
    expand_ref,
    key_ref,
    turned_ref,
    query_ref,
    rows_ref,
    wide,
    value_ref,
    gain_ref,
    norm_bias_ref,
    shrink_bias_ref,
    scale_ref,
    expand_bias_ref,
    sems,
):
    pairs = (
        (gain_hbm, gain_ref),
        (norm_bias_hbm, norm_bias_ref),
        (shrink_bias_hbm, shrink_bias_ref),
        (scale_hbm, scale_ref),
        (expand_bias_hbm, expand_bias_ref),
        (query_hbm, query_ref),
        (value_hbm, value_ref),
        (key_hbm, key_ref),
        *(
            (expand_hbm.at[k : k + LANES], expand_ref.at[k : k + LANES])
            for k in range(0, WIDTH, LANES)
        ),
    )
    copies = [pltpu.make_async_copy(s, d, sems.at[k]) for k, (s, d) in enumerate(pairs)]
    for copy in copies:
        copy.start()
    rows_ref[8:9, :] = bias_ref[...].reshape(1, WIDTH)
    for c in range(3):
        lanes = pl.ds(c * LANES, LANES)
        wide[c, :, 0:8, :] = jnp.zeros((CELLS_R, 8, LANES), jnp.float32)
        wide[c, :, 8 + CELLS_C : 16 + CELLS_C, :] = jnp.zeros((CELLS_R, 8, LANES), jnp.float32)
        wide[c, :, 8 : 8 + CELLS_C, :] = x_ref[:, :, lanes].astype(jnp.float32)

    def lane_tile(c, carry):
        lanes = pl.ds(pl.multiple_of(c * LANES, LANES), LANES)
        bias = jnp.broadcast_to(rows_ref[8:9, lanes], (8, LANES))
        for j in range(CELLS_C // 8):
            acc = [bias] * CELLS_R
            for b in range(7):
                at = 8 * j + 5 + b
                rows = [wide[c, r, at : at + 8, :] for r in range(CELLS_R)]
                acc = taps(acc, rows, weight_ref, lanes, b, 0)
            for i in range(CELLS_R):
                acc_ref[i, 8 * j : 8 * j + 8, lanes] = acc[i]
        return carry

    lax.fori_loop(0, 3, lane_tile, 0)
    for copy in copies:
        copy.wait()
    turned_ref[...] = value_ref[...].astype(jnp.float32).T.astype(jnp.bfloat16)
    for row, ref in enumerate((gain_ref, norm_bias_ref, shrink_bias_ref, scale_ref)):
        rows_ref[row : row + 1, :] = ref[...].reshape(1, WIDTH)
    for k in range(HID // WIDTH):
        rows_ref[4 + k : 5 + k, :] = expand_bias_ref[k * WIDTH : (k + 1) * WIDTH].reshape(1, WIDTH)


def halo_rows(acc_in, low_ref, high_ref, weight_ref, acc_ref, wide):
    for c in range(3):
        lanes = pl.ds(c * LANES, LANES)
        wide[c, :, 0:8, :] = jnp.zeros((6, 8, LANES), jnp.float32)
        wide[c, :, 8 + CELLS_C : 16 + CELLS_C, :] = jnp.zeros((6, 8, LANES), jnp.float32)
        wide[c, 0:3, 8 : 8 + CELLS_C, :] = low_ref[:, :, lanes].astype(jnp.float32)
        wide[c, 3:6, 8 : 8 + CELLS_C, :] = high_ref[:, :, lanes].astype(jnp.float32)

    def lane_tile(c, carry):
        lanes = pl.ds(pl.multiple_of(c * LANES, LANES), LANES)
        for j in range(CELLS_C // 8):
            acc = [acc_in[i, 8 * j : 8 * j + 8, lanes] for i in range(CELLS_R)]
            for b in range(7):
                at = 8 * j + 5 + b
                rows = [wide[c, r, at : at + 8, :] for r in range(6)]
                acc = taps(acc, rows[:3], weight_ref, lanes, b, -3)
                acc = taps(acc, rows[3:], weight_ref, lanes, b, CELLS_R)
            for i in range(CELLS_R):
                acc_ref[i, 8 * j : 8 * j + 8, lanes] = acc[i]
        return carry

    lax.fori_loop(0, 3, lane_tile, 0)


def halo_columns(acc_ref, left_ref, right_ref, weight_ref, edge):
    tall = CELLS_R + 6
    edge[...] = jnp.zeros(edge.shape, jnp.float32)
    for c in range(3):
        lanes = pl.ds(c * LANES, LANES)
        edge[0, c, :, 5:8, :] = left_ref[:, :, lanes].astype(jnp.float32)
        edge[1, c, :, 8:11, :] = right_ref[:, :, lanes].astype(jnp.float32)

    def lane_tile(c, carry):
        lanes = pl.ds(pl.multiple_of(c * LANES, LANES), LANES)
        for side in (0, 1):
            here = slice(8 * side, 8 * side + 8)
            acc = [acc_ref[i, here, lanes] for i in range(CELLS_R)]
            for b in (0, 1, 2) if side == 0 else (4, 5, 6):
                at = 5 + b if side == 0 else b - 3
                rows = [edge[side, c, r, at : at + 8, :] for r in range(tall)]
                acc = taps(acc, rows, weight_ref, lanes, b, -3)
            for i in range(CELLS_R):
                acc_ref[i, here, lanes] = acc[i]
        return carry

    lax.fori_loop(0, 3, lane_tile, 0)


def gelu(x):
    return 0.5 * x * (1.0 + lax.erf(x * (0.5**0.5)))


def block_of(conv_rows, inputs, lines_ref, expand_ref, shrink_ref, normed, hidden, copies=()):
    gain, norm_bias, shrink_bias, scale = (lines_ref[k : k + 1, :] for k in range(4))
    for i in range(CELLS_R):
        conv = conv_rows(i)
        center = jnp.mean(conv, axis=-1, keepdims=True)
        conv = conv - center
        variance = jnp.mean(conv * conv, axis=-1, keepdims=True)
        normed[i * HALF : (i + 1) * HALF, :] = (
            conv * lax.rsqrt(variance + 1e-06) * gain + norm_bias
        ).astype(jnp.bfloat16)
    for k in range(HID // WIDTH):
        lanes = slice(k * WIDTH, (k + 1) * WIDTH)
        part = jnp.dot(normed[...], expand_ref[:, lanes], preferred_element_type=jnp.float32)
        hidden[:, lanes] = gelu(part + lines_ref[4 + k : 5 + k, :]).astype(jnp.bfloat16)
    for copy in copies:
        copy.wait()
    shrunk = jnp.dot(hidden[...], shrink_ref[...], preferred_element_type=jnp.float32)
    shrunk = shrunk + shrink_bias
    inputs = inputs.reshape(CELLS_R * HALF, WIDTH).astype(jnp.float32)
    return (inputs + scale * shrunk).astype(jnp.bfloat16)


def keys_of(block, key_ref):
    return jnp.dot(block, key_ref[...], preferred_element_type=jnp.float32).astype(jnp.bfloat16)


def values_of(block, turned_ref):
    return lax.dot_general(
        turned_ref[...], block, (((1,), (1,)), ((), ())), preferred_element_type=jnp.float32
    ).astype(jnp.bfloat16)


def inner_kernel(
    acc_in,
    low_ref,
    high_ref,
    weight_ref,
    x_ref,
    lines_ref,
    expand_ref,
    shrink_hbm,
    key_ref,
    turned_ref,
    query_ref,
    sides_ref,
    block_ref,
    keys_ref,
    values_ref,
    shrink_ref,
    big_ref,
    wide,
    acc_ref,
    normed,
    hidden,
    sems,
):
    copies = [
        pltpu.make_async_copy(
            shrink_hbm.at[k * WIDTH : (k + 1) * WIDTH],
            shrink_ref.at[k * WIDTH : (k + 1) * WIDTH],
            sems.at[k],
        )
        for k in range(HID // WIDTH)
    ]
    for copy in copies:
        copy.start()
    halo_rows(acc_in, low_ref, high_ref, weight_ref, acc_ref, wide)
    query = query_ref[...].astype(jnp.float32)
    query = jnp.concatenate([query, query], axis=0).T
    head = lax.broadcasted_iota(jnp.int32, (WIDTH, LANES), 0) // (WIDTH // NH)
    half = lax.broadcasted_iota(jnp.int32, (WIDTH, LANES), 1) // NQ
    for t in range(NH // 2):
        big_ref[:, t * LANES : (t + 1) * LANES] = jnp.where(
            head == 2 * t + half, query, 0.0
        ).astype(jnp.bfloat16)
    sides_ref[:, 0:8, :] = acc_ref[:, 0:8, :]
    sides_ref[:, 8:16, :] = acc_ref[:, CELLS_C - 8 : CELLS_C, :]
    block = block_of(
        lambda i: acc_ref[i, 8 : 8 + HALF, :],
        x_ref[:, 8 : 8 + HALF, :],
        lines_ref,
        expand_ref,
        shrink_ref,
        normed,
        hidden,
        copies,
    )
    block_ref[...] = block.reshape(CELLS_R, HALF, WIDTH)
    keys_ref[...] = keys_of(block, key_ref)
    values_ref[...] = values_of(block, turned_ref)


def marked(weighted, marks):
    high = marks.astype(jnp.bfloat16).astype(jnp.float32)
    rest = marks - high
    middle = rest.astype(jnp.bfloat16).astype(jnp.float32)
    low = (rest - middle).astype(jnp.bfloat16).astype(jnp.float32)
    marks = high + pltpu.roll(middle, NH, 1) + pltpu.roll(low, 2 * NH, 1)
    lane = lax.broadcasted_iota(jnp.int32, marks.shape, 1)
    last = jnp.where(lane < MARK, weighted[:, LANES:], marks)
    return jnp.concatenate([weighted[:, :LANES], last], axis=1).astype(jnp.bfloat16)


def outer_kernel(
    tissue_ref,
    acc_in,
    left_ref,
    right_ref,
    weight_ref,
    x_ref,
    lines_ref,
    expand_ref,
    shrink_ref,
    key_ref,
    turned_ref,
    big_ref,
    block_ref,
    keys_ref,
    values_ref,
    out_ref,
    part_ref,
    acc_ref,
    edge,
    normed,
    hidden,
    sums,
    whole,
    sem,
):
    acc_ref[...] = acc_in[...]
    whole[:, 8 : 8 + HALF, :] = block_ref[...]
    halo_columns(acc_ref, left_ref, right_ref, weight_ref, edge)
    block = block_of(
        lambda i: acc_ref[i],
        jnp.concatenate([x_ref[:, 0:8, :], x_ref[:, CELLS_C - 8 : CELLS_C, :]], axis=1),
        lines_ref,
        expand_ref,
        shrink_ref,
        normed,
        hidden,
    )
    parts = block.reshape(CELLS_R, HALF, WIDTH)
    whole[:, 0:8, :] = parts[:, 0:8, :]
    whole[:, CELLS_C - 8 : CELLS_C, :] = parts[:, 8:16, :]
    copy = pltpu.make_async_copy(whole, out_ref, sem)
    copy.start()
    keys = jnp.concatenate([keys_ref[...], keys_of(block, key_ref)], axis=0)
    values = jnp.concatenate([values_ref[...], values_of(block, turned_ref)], axis=1)
    size = WIDTH // NH
    tiles = ((1, 2), (0, 3))
    live = [[tissue_ref[0, t] > 0 for t in pair] for pair in tiles]
    line = lax.broadcasted_iota(jnp.int32, (NH, LANES), 0)
    tops = jnp.zeros((NH, LANES), jnp.float32)
    totals = jnp.zeros((NH, LANES), jnp.float32)
    scores = jnp.dot(keys, big_ref[...], preferred_element_type=jnp.float32)
    scores = (scores * (size**-0.5 * LOG2E)).reshape(2, CELLS_R, 2, TILE, NH * NQ)
    scores = [[jnp.where(live[h][g], scores[h, :, g], -1e30) for g in range(2)] for h in range(2)]
    all_top = jnp.maximum(
        jnp.maximum(scores[0][0], scores[0][1]), jnp.maximum(scores[1][0], scores[1][1])
    )
    all_top = jnp.ceil(jnp.max(jnp.max(all_top, axis=0), axis=0, keepdims=True))
    weights = [
        [jnp.where(live[h][g], jnp.exp2(scores[h][g] - all_top), 0.0) for g in range(2)]
        for h in range(2)
    ]
    all_total = (weights[0][0] + weights[0][1]) + (weights[1][0] + weights[1][1])
    all_total = jnp.sum(jnp.sum(all_total, axis=0), axis=0, keepdims=True)
    weights = [jnp.stack(pair, axis=1).reshape(CELLS_R * HALF, NH * NQ) for pair in weights]
    weights = jnp.concatenate(weights, axis=0).astype(jnp.bfloat16)
    for t in range(NH // 2):
        lanes = slice(t * LANES, (t + 1) * LANES)
        top, total = all_top[:, lanes], all_total[:, lanes]
        pair = jnp.dot(
            values[2 * size * t : 2 * size * (t + 1), :],
            weights[:, lanes],
            preferred_element_type=jnp.float32,
        )
        at = 2 * size * t + (t // 2) * (256 - SHARE)
        sums[at : at + size, :] = pair[:size]
        sums[at + size : at + 2 * size, :] = pltpu.roll(pair[size:], NQ, 1)
        top = jnp.broadcast_to(top, (NH, LANES))
        total = jnp.broadcast_to(total, (NH, LANES))
        tops = jnp.where(line == 2 * t, top, tops)
        tops = jnp.where(line == 2 * t + 1, pltpu.roll(top, NQ, 1), tops)
        totals = jnp.where(line == 2 * t, total, totals)
        totals = jnp.where(line == 2 * t + 1, pltpu.roll(total, NQ, 1), totals)
    for u in range(2):
        at = 256 * u + SHARE
        sums[at : at + 64, :] = jnp.zeros((64, LANES), jnp.float32)
        sums[at : at + NH, :] = pltpu.roll(tops, 4, 0) if u else tops
        sums[at + 3 * NH : at + 4 * NH, :] = pltpu.roll(totals, 4, 0) if u else totals
    part = sums[...].T
    for u in range(2):
        share = part[:NQ, 256 * u : 256 * (u + 1)]
        lane = lax.broadcasted_iota(jnp.int32, (NQ, LANES), 1)
        part_ref[u] = marked(share, jnp.where(lane < MARK, 0.0, share[:, LANES:]))
    copy.wait()


def spread_matrix(first, copies):
    lane = lax.broadcasted_iota(jnp.int32, (LANES, 256), 0) - first
    head = lax.broadcasted_iota(jnp.int32, (LANES, 256), 1) // (WIDTH // NH)
    inside = (lane >= 0) & (lane < copies * NH) & (head < 4)
    return jnp.where(inside & (lane % NH == head), 1.0, 0.0).astype(jnp.bfloat16)


def merge_kernel(parts_ref, out_ref):
    n, q, width = parts_ref.shape
    parts = parts_ref[...].astype(jnp.float32)
    lane = lax.broadcasted_iota(jnp.int32, (n * q, LANES), 1)
    marks = parts[:, :, LANES:].reshape(n * q, LANES)
    marks = jnp.where(lane < MARK, 0.0, marks)
    marks = marks + pltpu.roll(marks, LANES - NH, 1) + pltpu.roll(marks, LANES - 2 * NH, 1)
    top = jnp.max(marks.reshape(n, q, LANES), axis=0)
    factor = jnp.exp2(marks.reshape(n, q, LANES) - top).reshape(n * q, LANES)
    factor = factor.astype(jnp.bfloat16)
    spread = jnp.dot(factor, spread_matrix(MARK, 1), preferred_element_type=jnp.float32)
    weighted = jnp.sum(parts * spread.reshape(n, q, width), axis=0)
    total = marks * pltpu.roll(factor.astype(jnp.float32), 3 * NH, 1)
    total = jnp.sum(total.reshape(n, q, LANES), axis=0)
    lane = lane[:q]
    part = jnp.where((lane >= MARK) & (lane < MARK + 4), top, 0.0)
    part = jnp.where((lane >= MARK + 3 * NH) & (lane < MARK + 3 * NH + 4), total, part)
    share = marked(weighted, part)
    out_ref[...] = jnp.broadcast_to(share[None], out_ref.shape)


def pool_kernel(parts_ref, class_ref, label_ref, out_ref, loss_ref):
    parts = parts_ref[...].reshape(2 * NQ, 256).astype(jnp.float32)
    lane = lax.broadcasted_iota(jnp.int32, (2 * NQ, LANES), 1)
    first = MARK + 3 * NH
    marks = jnp.where(lane < MARK, 0.0, parts[:, LANES:])
    marks = marks + pltpu.roll(marks, LANES - NH, 1) + pltpu.roll(marks, LANES - 2 * NH, 1)
    inside = (lane >= first) & (lane < first + 4)
    marks = jnp.where(inside, 1.0 / jnp.where(inside, marks, 1.0), 0.0)
    marks = marked(parts, marks)[:, LANES:]
    inverse = jnp.dot(marks, spread_matrix(first, 3), preferred_element_type=jnp.float32)
    pooled = (parts * inverse).reshape(2, NQ, 256)
    pooled = jnp.concatenate([pooled[0, :, :SHARE], pooled[1, :, :SHARE]], axis=1)
    out_ref[...] = pooled
    lines = jnp.sum(pooled.reshape(NQ // 8, 8, WIDTH), axis=0)
    logits = lax.dot_general(
        lines,
        class_ref[...],
        (((1,), (1,)), ((), ())),
        precision=lax.Precision.HIGHEST,
        preferred_element_type=jnp.float32,
    )
    logits = jnp.sum(logits, axis=0, keepdims=True)
    label = label_ref[...].reshape(logits.shape).astype(jnp.float32)
    soft = jnp.maximum(logits, 0.0) + jnp.log1p(jnp.exp(-jnp.abs(logits)))
    loss_ref[0] = jnp.sum(soft - label * logits)


def everyone(part, groups):
    return lax.all_to_all(part, ("row", "col"), 0, 0, axis_index_groups=groups, tiled=True)


def call(kernel, out_shape, name, *args, **more):
    return pl.pallas_call(kernel, out_shape=out_shape, name=name, **more, **params())(*args)


def merged(part, class_weight, slide_label):
    rest, shares = (jax.ShapeDtypeStruct((n, NQ // 8, 256), jnp.bfloat16) for n in (32, 16))
    parts = everyone(part.reshape(shares.shape), SHARES)
    parts = everyone(call(merge_kernel, rest, "merge_first", parts), REST)
    parts = everyone(call(merge_kernel, shares, "merge_second", parts), SHARES)
    return call(
        pool_kernel,
        (jax.ShapeDtypeStruct((NQ, WIDTH), jnp.float32), jax.ShapeDtypeStruct((1,), jnp.float32)),
        "pool",
        parts,
        class_weight.T,
        slide_label,
        out_specs=(pl.BlockSpec(memory_space=pltpu.VMEM), pl.BlockSpec(memory_space=pltpu.SMEM)),
    )


def vmem(*shape):
    return pltpu.VMEM(shape, jnp.float32)


def params(flops=1000000):
    return dict(
        compiler_params=pltpu.CompilerParams(vmem_limit_bytes=24 * 1024 * 1024),
        cost_estimate=pl.CostEstimate(flops=flops, bytes_accessed=1000000, transcendentals=0),
    )


def swapped(near, far, axis):
    count, odd = lax.axis_size(axis), lax.axis_index(axis) % 2 == 1
    inner = [(i, i ^ 1) for i in range(count)]
    outer = [(i, i + 1 if i % 2 else i - 1) for i in range(1, count - 1)]
    near, far = lax.ppermute(near, axis, inner), lax.ppermute(far, axis, outer)
    return jnp.where(odd, near, far), jnp.where(odd, far, near)


def exchanged(first, last, axis):
    odd = lax.axis_index(axis) % 2 == 1
    return swapped(jnp.where(odd, first, last), jnp.where(odd, last, first), axis)


def per_device(
    features,
    depth_weight,
    depth_bias,
    norm_gain,
    norm_bias,
    expand_weight,
    expand_bias,
    shrink_weight,
    shrink_bias,
    layer_scale,
    key_weight,
    value_weight,
    queries,
    class_weight,
    tissue,
    slide_label,
):
    rows, cols, width = features.shape
    f32, bf16 = jnp.float32, jnp.bfloat16
    hbm, whole = pl.BlockSpec(memory_space=pltpu.HBM), pl.BlockSpec(memory_space=pltpu.VMEM)
    shaped = jax.ShapeDtypeStruct
    cells, taps_, bias, near, far, first, last = call(
        fetch_kernel,
        (
            shaped(features.shape, bf16),
            shaped(depth_weight.shape, f32),
            shaped(depth_bias.shape, f32),
            *[shaped((3, cols, width), bf16)] * 2,
            *[shaped((rows, 3, width), bf16)] * 2,
        ),
        "fetch_cells",
        *(
            pltpu.with_memory_space_constraint(array, pltpu.HBM)
            for array in (features, depth_weight, depth_bias)
        ),
        in_specs=[hbm] * 3,
        out_specs=(whole,) * 7,
        scratch_shapes=[pltpu.SemaphoreType.DMA((3,))],
    )
    low, high = swapped(near, far, "row")
    acc, expand, key, turned, query, lines = call(
        own_kernel,
        (
            shaped((rows, cols, width), f32),
            shaped(expand_weight.shape, bf16),
            shaped(key_weight.shape, bf16),
            shaped(value_weight.shape, bf16),
            shaped(queries.shape, bf16),
            shaped((16, width), f32),
        ),
        "own_cells",
        cells,
        taps_,
        bias,
        *(
            pltpu.with_memory_space_constraint(array, pltpu.HBM)
            for array in (
                expand_weight,
                key_weight,
                value_weight,
                queries,
                norm_gain,
                norm_bias,
                shrink_bias,
                layer_scale,
                expand_bias,
            )
        ),
        in_specs=[whole] * 3 + [hbm] * 9,
        out_specs=(whole,) * 6,
        scratch_shapes=[
            vmem(3, rows, cols + 16, LANES),
            pltpu.VMEM(value_weight.shape, bf16),
            *(vmem(width) for _ in range(4)),
            vmem(HID),
            pltpu.SemaphoreType.DMA((11,)),
        ],
    )
    first, last, acc = lax.optimization_barrier((first, last, acc))
    left, right = exchanged(
        jnp.concatenate([low[:, :3], first, high[:, :3]], axis=0),
        jnp.concatenate([low[:, -3:], last, high[:, -3:]], axis=0),
        "col",
    )
    count = rows * HALF
    work = [pltpu.VMEM((count, width), bf16), pltpu.VMEM((count, HID), bf16)]
    sides, inner, keys, values, shrink, big = call(
        inner_kernel,
        (
            shaped((rows, HALF, width), f32),
            shaped((rows, HALF, width), bf16),
            shaped((count, width), bf16),
            shaped((width, count), bf16),
            shaped(shrink_weight.shape, bf16),
            shaped((width, NH * NQ), bf16),
        ),
        "inner_cells",
        acc,
        low,
        high,
        taps_,
        cells,
        lines,
        expand,
        pltpu.with_memory_space_constraint(shrink_weight, pltpu.HBM),
        key,
        turned,
        query,
        in_specs=[whole] * 7 + [hbm] + [whole] * 3,
        out_specs=(whole,) * 6,
        scratch_shapes=[
            vmem(3, 6, cols + 16, LANES),
            vmem(rows, cols, width),
            *work,
            pltpu.SemaphoreType.DMA((HID // width,)),
        ],
    )
    block_out, part = call(
        outer_kernel,
        (shaped((rows, cols, width), bf16), shaped((2, NQ, 256), bf16)),
        "outer_cells",
        tissue,
        sides,
        left,
        right,
        taps_,
        cells,
        lines,
        expand,
        shrink,
        key,
        turned,
        big,
        inner,
        keys,
        values,
        in_specs=[pl.BlockSpec(memory_space=pltpu.SMEM)] + [whole] * 14,
        out_specs=(hbm, whole),
        scratch_shapes=[
            vmem(rows, HALF, width),
            vmem(2, 3, rows + 6, 16, LANES),
            *work,
            vmem(width + LANES, LANES),
            pltpu.VMEM((rows, cols, width), bf16),
            pltpu.SemaphoreType.DMA,
        ],
    )
    pooled, slide_loss = merged(part, class_weight, slide_label)
    return (block_out, pooled, slide_loss)


def solution(mesh):
    placed = (P("row", "col", None),) + (P(),) * 13 + (P("row", "col"), P())
    return jax.shard_map(
        per_device,
        mesh=mesh,
        in_specs=placed,
        out_specs=(P("row", "col", None), P(), P()),
        check_vma=False,
    )
```

```python
import jax
import jax.numpy as jnp
from jax import lax
from jax.experimental import pallas as pl
from jax.experimental.pallas import tpu as pltpu
from jax.sharding import PartitionSpec as P

NH = 8
NQ = 64
TILE = 8
LOG2E = 1.4426950408889634


def device(z, near, y):
    return (z * 8 + near) * 8 + y


EIGHT, FOUR, TWO = range(8), range(4), range(2)
SHARES = [[device(2 * z + k, n, y) for k in TWO for n in EIGHT] for z in FOUR for y in EIGHT]
REST = [[device(2 * z + k, n, y) for z in FOUR for y in EIGHT] for k in TWO for n in EIGHT]
WIDTH = 384
LANES = 128
CELLS_R = 8
CELLS_C = 32
HID = 1536
HALF = 16
SHARE = 192
MARK = SHARE - LANES


def taps(acc, rows, weight_ref, lanes, b, first):
    for a in range(7):
        weight = weight_ref[a, b : b + 1, lanes]
        for i in range(CELLS_R):
            at = i + a - 3 - first
            if 0 <= at < len(rows):
                acc[i] = acc[i] + rows[at] * weight
    return acc


def fetch_kernel(
    x_hbm, weight_hbm, bias_hbm, x_ref, weight_ref, bias_ref, inner_ref, outer_ref, first_ref, last_ref, sems
):
    pairs = ((x_hbm, x_ref), (weight_hbm, weight_ref), (bias_hbm, bias_ref))
    copies = [pltpu.make_async_copy(s, d, sems.at[k]) for k, (s, d) in enumerate(pairs)]
    for copy in copies:
        copy.start()
    copies[0].wait()
    odd = lax.axis_index("row") % 2
    inner_ref[...] = x_ref[pl.ds((1 - odd) * (CELLS_R - 3), 3)]
    outer_ref[...] = x_ref[pl.ds(odd * (CELLS_R - 3), 3)]
    first_ref[...] = x_ref[:, 0:3, :]
    last_ref[...] = x_ref[:, CELLS_C - 3 : CELLS_C, :]
    for copy in copies[1:]:
        copy.wait()


def own_kernel(
    x_ref,
    weight_ref,
    bias_ref,
    expand_hbm,
    query_hbm,
    gain_hbm,
    norm_bias_hbm,
    shrink_bias_hbm,
    scale_hbm,
    expand_bias_hbm,
    acc_ref,
    expand_ref,
    query_ref,
    rows_ref,
    wide,
    gain_ref,
    norm_bias_ref,
    shrink_bias_ref,
    scale_ref,
    expand_bias_ref,
    sems,
):
    pairs = (
        (gain_hbm, gain_ref),
        (norm_bias_hbm, norm_bias_ref),
        (shrink_bias_hbm, shrink_bias_ref),
        (scale_hbm, scale_ref),
        (expand_bias_hbm, expand_bias_ref),
        (query_hbm, query_ref),
        *(
            (expand_hbm.at[k : k + LANES], expand_ref.at[k : k + LANES])
            for k in range(0, WIDTH, LANES)
        ),
    )
    copies = [pltpu.make_async_copy(s, d, sems.at[k]) for k, (s, d) in enumerate(pairs)]
    for copy in copies:
        copy.start()
    rows_ref[8:9, :] = bias_ref[...].reshape(1, WIDTH)
    groups = CELLS_C // 8
    for c in range(3):
        cells = x_ref[:, :, pl.ds(c * LANES, LANES)].astype(jnp.float32)
        for j in range(groups):
            for k in range(3):
                at = 8 * (j + k - 1)
                part = jnp.zeros((CELLS_R, 8, LANES), jnp.float32)
                if 0 <= at < CELLS_C:
                    part = cells[:, at : at + 8]
                wide[groups * c + j, :, 8 * k : 8 * k + 8, :] = part

    def lane_tile(step, carry):
        c, j = step // groups, step % groups
        lanes = pl.ds(pl.multiple_of(c * LANES, LANES), LANES)
        acc = [jnp.broadcast_to(rows_ref[8:9, lanes], (8, LANES))] * CELLS_R
        for b in range(7):
            rows = [wide[step, r, 5 + b : 13 + b, :] for r in range(CELLS_R)]
            acc = taps(acc, rows, weight_ref, lanes, b, 0)
        for i in range(CELLS_R):
            acc_ref[i, pl.ds(pl.multiple_of(8 * j, 8), 8), lanes] = acc[i]
        return carry

    lax.fori_loop(0, 3 * groups, lane_tile, 0)
    for copy in copies:
        copy.wait()
    for row, ref in enumerate((gain_ref, norm_bias_ref, shrink_bias_ref, scale_ref)):
        rows_ref[row : row + 1, :] = ref[...].reshape(1, WIDTH)
    for k in range(HID // WIDTH):
        rows_ref[4 + k : 5 + k, :] = expand_bias_ref[k * WIDTH : (k + 1) * WIDTH].reshape(1, WIDTH)


def halo_rows(acc_in, low_ref, high_ref, weight_ref, acc_ref, wide):
    for c in range(3):
        lanes = pl.ds(c * LANES, LANES)
        wide[c, :, 0:8, :] = jnp.zeros((6, 8, LANES), jnp.float32)
        wide[c, :, 8 + CELLS_C : 16 + CELLS_C, :] = jnp.zeros((6, 8, LANES), jnp.float32)
        wide[c, 0:3, 8 : 8 + CELLS_C, :] = low_ref[:, :, lanes].astype(jnp.float32)
        wide[c, 3:6, 8 : 8 + CELLS_C, :] = high_ref[:, :, lanes].astype(jnp.float32)

    def lane_tile(c, carry):
        lanes = pl.ds(pl.multiple_of(c * LANES, LANES), LANES)
        for j in range(CELLS_C // 8):
            acc = [acc_in[i, 8 * j : 8 * j + 8, lanes] for i in range(CELLS_R)]
            for b in range(7):
                at = 8 * j + 5 + b
                rows = [wide[c, r, at : at + 8, :] for r in range(6)]
                acc = taps(acc, rows[:3], weight_ref, lanes, b, -3)
                acc = taps(acc, rows[3:], weight_ref, lanes, b, CELLS_R)
            for i in range(CELLS_R):
                acc_ref[i, 8 * j : 8 * j + 8, lanes] = acc[i]
        return carry

    lax.fori_loop(0, 3, lane_tile, 0)


def halo_columns(acc_ref, left_ref, right_ref, weight_ref, edge):
    tall = CELLS_R + 6
    edge[...] = jnp.zeros(edge.shape, jnp.float32)
    for c in range(3):
        lanes = pl.ds(c * LANES, LANES)
        edge[0, c, :, 5:8, :] = left_ref[:, :, lanes].astype(jnp.float32)
        edge[1, c, :, 8:11, :] = right_ref[:, :, lanes].astype(jnp.float32)

    def lane_tile(c, carry):
        lanes = pl.ds(pl.multiple_of(c * LANES, LANES), LANES)
        for side in (0, 1):
            here = slice(8 * side, 8 * side + 8)
            acc = [acc_ref[i, here, lanes] for i in range(CELLS_R)]
            for b in (0, 1, 2) if side == 0 else (4, 5, 6):
                at = 5 + b if side == 0 else b - 3
                rows = [edge[side, c, r, at : at + 8, :] for r in range(tall)]
                acc = taps(acc, rows, weight_ref, lanes, b, -3)
            for i in range(CELLS_R):
                acc_ref[i, here, lanes] = acc[i]
        return carry

    lax.fori_loop(0, 3, lane_tile, 0)


def gelu(x):
    return 0.5 * x * (1.0 + lax.erf(x * (0.5**0.5)))


def block_of(conv_rows, inputs, lines_ref, expand_ref, shrink_ref, normed, hidden, copies=()):
    gain, norm_bias, shrink_bias, scale = (lines_ref[k : k + 1, :] for k in range(4))
    for i in range(CELLS_R):
        conv = conv_rows(i)
        center = jnp.mean(conv, axis=-1, keepdims=True)
        conv = conv - center
        variance = jnp.mean(conv * conv, axis=-1, keepdims=True)
        normed[i * HALF : (i + 1) * HALF, :] = (
            conv * lax.rsqrt(variance + 1e-06) * gain + norm_bias
        ).astype(jnp.bfloat16)
    for k in range(HID // WIDTH):
        lanes = slice(k * WIDTH, (k + 1) * WIDTH)
        part = jnp.dot(normed[...], expand_ref[:, lanes], preferred_element_type=jnp.float32)
        hidden[:, lanes] = gelu(part + lines_ref[4 + k : 5 + k, :]).astype(jnp.bfloat16)
    for copy in copies:
        copy.wait()
    shrunk = jnp.dot(hidden[...], shrink_ref[...], preferred_element_type=jnp.float32)
    shrunk = shrunk + shrink_bias
    inputs = inputs.reshape(CELLS_R * HALF, WIDTH).astype(jnp.float32)
    return (inputs + scale * shrunk).astype(jnp.bfloat16)


def keys_of(block, key_ref):
    return jnp.dot(block, key_ref[...], preferred_element_type=jnp.float32).astype(jnp.bfloat16)


def values_of(block, turned_ref):
    return lax.dot_general(
        turned_ref[...], block, (((1,), (1,)), ((), ())), preferred_element_type=jnp.float32
    ).astype(jnp.bfloat16)


def inner_kernel(
    acc_in,
    low_ref,
    high_ref,
    weight_ref,
    x_ref,
    lines_ref,
    expand_ref,
    shrink_hbm,
    key_hbm,
    value_hbm,
    query_ref,
    sides_ref,
    block_ref,
    keys_ref,
    values_ref,
    shrink_ref,
    key_ref,
    turned_ref,
    big_ref,
    wide,
    acc_ref,
    normed,
    hidden,
    value_ref,
    sems,
):
    copies = [
        pltpu.make_async_copy(
            shrink_hbm.at[k * WIDTH : (k + 1) * WIDTH],
            shrink_ref.at[k * WIDTH : (k + 1) * WIDTH],
            sems.at[k],
        )
        for k in range(HID // WIDTH)
    ]
    late = [
        pltpu.make_async_copy(value_hbm, value_ref, sems.at[4]),
        pltpu.make_async_copy(key_hbm, key_ref, sems.at[5]),
    ]
    for copy in copies + late:
        copy.start()
    halo_rows(acc_in, low_ref, high_ref, weight_ref, acc_ref, wide)
    for copy in late:
        copy.wait()
    turned_ref[...] = value_ref[...].astype(jnp.float32).T.astype(jnp.bfloat16)
    query = query_ref[...].astype(jnp.float32)
    query = jnp.concatenate([query, query], axis=0).T
    head = lax.broadcasted_iota(jnp.int32, (WIDTH, LANES), 0) // (WIDTH // NH)
    half = lax.broadcasted_iota(jnp.int32, (WIDTH, LANES), 1) // NQ
    for t in range(NH // 2):
        big_ref[:, t * LANES : (t + 1) * LANES] = jnp.where(
            head == 2 * t + half, query, 0.0
        ).astype(jnp.bfloat16)
    sides_ref[:, 0:8, :] = acc_ref[:, 0:8, :]
    sides_ref[:, 8:16, :] = acc_ref[:, CELLS_C - 8 : CELLS_C, :]
    block = block_of(
        lambda i: acc_ref[i, 8 : 8 + HALF, :],
        x_ref[:, 8 : 8 + HALF, :],
        lines_ref,
        expand_ref,
        shrink_ref,
        normed,
        hidden,
        copies,
    )
    block_ref[...] = block.reshape(CELLS_R, HALF, WIDTH)
    keys_ref[...] = keys_of(block, key_ref)
    values_ref[...] = values_of(block, turned_ref)


def marked(weighted, marks):
    high = marks.astype(jnp.bfloat16).astype(jnp.float32)
    rest = marks - high
    middle = rest.astype(jnp.bfloat16).astype(jnp.float32)
    low = (rest - middle).astype(jnp.bfloat16).astype(jnp.float32)
    marks = high + pltpu.roll(middle, NH, 1) + pltpu.roll(low, 2 * NH, 1)
    lane = lax.broadcasted_iota(jnp.int32, marks.shape, 1)
    last = jnp.where(lane < MARK, weighted[:, LANES:], marks)
    return jnp.concatenate([weighted[:, :LANES], last], axis=1).astype(jnp.bfloat16)


def outer_kernel(
    tissue_ref,
    acc_in,
    left_ref,
    right_ref,
    weight_ref,
    x_ref,
    lines_ref,
    expand_ref,
    shrink_ref,
    key_ref,
    turned_ref,
    big_ref,
    block_ref,
    keys_ref,
    values_ref,
    out_ref,
    part_ref,
    acc_ref,
    edge,
    normed,
    hidden,
    sums,
    whole,
    sem,
):
    acc_ref[...] = acc_in[...]
    whole[:, 8 : 8 + HALF, :] = block_ref[...]
    halo_columns(acc_ref, left_ref, right_ref, weight_ref, edge)
    block = block_of(
        lambda i: acc_ref[i],
        jnp.concatenate([x_ref[:, 0:8, :], x_ref[:, CELLS_C - 8 : CELLS_C, :]], axis=1),
        lines_ref,
        expand_ref,
        shrink_ref,
        normed,
        hidden,
    )
    parts = block.reshape(CELLS_R, HALF, WIDTH)
    whole[:, 0:8, :] = parts[:, 0:8, :]
    whole[:, CELLS_C - 8 : CELLS_C, :] = parts[:, 8:16, :]
    copy = pltpu.make_async_copy(whole, out_ref, sem)
    copy.start()
    keys = jnp.concatenate([keys_ref[...], keys_of(block, key_ref)], axis=0)
    values = jnp.concatenate([values_ref[...], values_of(block, turned_ref)], axis=1)
    size = WIDTH // NH
    tiles = ((1, 2), (0, 3))
    live = [[tissue_ref[0, t] > 0 for t in pair] for pair in tiles]
    line = lax.broadcasted_iota(jnp.int32, (NH, LANES), 0)
    tops = jnp.zeros((NH, LANES), jnp.float32)
    totals = jnp.zeros((NH, LANES), jnp.float32)
    scores = jnp.dot(keys, big_ref[...], preferred_element_type=jnp.float32)
    scores = (scores * (size**-0.5 * LOG2E)).reshape(2, CELLS_R, 2, TILE, NH * NQ)
    scores = [[jnp.where(live[h][g], scores[h, :, g], -1e30) for g in range(2)] for h in range(2)]
    all_top = jnp.maximum(
        jnp.maximum(scores[0][0], scores[0][1]), jnp.maximum(scores[1][0], scores[1][1])
    )
    all_top = jnp.ceil(jnp.max(jnp.max(all_top, axis=0), axis=0, keepdims=True))
    weights = [
        [jnp.where(live[h][g], jnp.exp2(scores[h][g] - all_top), 0.0) for g in range(2)]
        for h in range(2)
    ]
    all_total = (weights[0][0] + weights[0][1]) + (weights[1][0] + weights[1][1])
    all_total = jnp.sum(jnp.sum(all_total, axis=0), axis=0, keepdims=True)
    weights = [jnp.stack(pair, axis=1).reshape(CELLS_R * HALF, NH * NQ) for pair in weights]
    weights = jnp.concatenate(weights, axis=0).astype(jnp.bfloat16)
    for t in range(NH // 2):
        lanes = slice(t * LANES, (t + 1) * LANES)
        top, total = all_top[:, lanes], all_total[:, lanes]
        pair = jnp.dot(
            values[2 * size * t : 2 * size * (t + 1), :],
            weights[:, lanes],
            preferred_element_type=jnp.float32,
        )
        at = 2 * size * t + (t // 2) * (256 - SHARE)
        sums[at : at + size, :] = pair[:size]
        sums[at + size : at + 2 * size, :] = pltpu.roll(pair[size:], NQ, 1)
        top = jnp.broadcast_to(top, (NH, LANES))
        total = jnp.broadcast_to(total, (NH, LANES))
        tops = jnp.where(line == 2 * t, top, tops)
        tops = jnp.where(line == 2 * t + 1, pltpu.roll(top, NQ, 1), tops)
        totals = jnp.where(line == 2 * t, total, totals)
        totals = jnp.where(line == 2 * t + 1, pltpu.roll(total, NQ, 1), totals)
    for u in range(2):
        at = 256 * u + SHARE
        sums[at : at + 64, :] = jnp.zeros((64, LANES), jnp.float32)
        sums[at : at + NH, :] = pltpu.roll(tops, 4, 0) if u else tops
        sums[at + 3 * NH : at + 4 * NH, :] = pltpu.roll(totals, 4, 0) if u else totals
    part = sums[...].T
    for u in range(2):
        share = part[:NQ, 256 * u : 256 * (u + 1)]
        lane = lax.broadcasted_iota(jnp.int32, (NQ, LANES), 1)
        part_ref[u] = marked(share, jnp.where(lane < MARK, 0.0, share[:, LANES:]))
    copy.wait()


def spread_matrix(first, copies):
    lane = lax.broadcasted_iota(jnp.int32, (LANES, 256), 0) - first
    head = lax.broadcasted_iota(jnp.int32, (LANES, 256), 1) // (WIDTH // NH)
    inside = (lane >= 0) & (lane < copies * NH) & (head < 4)
    return jnp.where(inside & (lane % NH == head), 1.0, 0.0).astype(jnp.bfloat16)


def merge_kernel(parts_ref, out_ref):
    n, q, width = parts_ref.shape
    parts = parts_ref[...].astype(jnp.float32)
    lane = lax.broadcasted_iota(jnp.int32, (n * q, LANES), 1)
    marks = parts[:, :, LANES:].reshape(n * q, LANES)
    marks = jnp.where(lane < MARK, 0.0, marks)
    marks = marks + pltpu.roll(marks, LANES - NH, 1) + pltpu.roll(marks, LANES - 2 * NH, 1)
    top = jnp.max(marks.reshape(n, q, LANES), axis=0)
    factor = jnp.exp2(marks.reshape(n, q, LANES) - top).reshape(n * q, LANES)
    factor = factor.astype(jnp.bfloat16)
    spread = jnp.dot(factor, spread_matrix(MARK, 1), preferred_element_type=jnp.float32)
    weighted = jnp.sum(parts * spread.reshape(n, q, width), axis=0)
    total = marks * pltpu.roll(factor.astype(jnp.float32), 3 * NH, 1)
    total = jnp.sum(total.reshape(n, q, LANES), axis=0)
    lane = lane[:q]
    part = jnp.where((lane >= MARK) & (lane < MARK + 4), top, 0.0)
    part = jnp.where((lane >= MARK + 3 * NH) & (lane < MARK + 3 * NH + 4), total, part)
    share = marked(weighted, part)
    out_ref[...] = jnp.broadcast_to(share[None], out_ref.shape)


def pool_kernel(parts_ref, class_ref, label_ref, out_ref, loss_ref):
    parts = parts_ref[...].reshape(2 * NQ, 256).astype(jnp.float32)
    lane = lax.broadcasted_iota(jnp.int32, (2 * NQ, LANES), 1)
    first = MARK + 3 * NH
    marks = jnp.where(lane < MARK, 0.0, parts[:, LANES:])
    marks = marks + pltpu.roll(marks, LANES - NH, 1) + pltpu.roll(marks, LANES - 2 * NH, 1)
    inside = (lane >= first) & (lane < first + 4)
    marks = jnp.where(inside, 1.0 / jnp.where(inside, marks, 1.0), 0.0)
    marks = marked(parts, marks)[:, LANES:]
    inverse = jnp.dot(marks, spread_matrix(first, 3), preferred_element_type=jnp.float32)
    pooled = (parts * inverse).reshape(2, NQ, 256)
    pooled = jnp.concatenate([pooled[0, :, :SHARE], pooled[1, :, :SHARE]], axis=1)
    out_ref[...] = pooled
    lines = jnp.sum(pooled.reshape(NQ // 8, 8, WIDTH), axis=0)
    logits = lax.dot_general(
        lines,
        class_ref[...],
        (((1,), (1,)), ((), ())),
        precision=lax.Precision.HIGHEST,
        preferred_element_type=jnp.float32,
    )
    logits = jnp.sum(logits, axis=0, keepdims=True)
    label = label_ref[...].reshape(logits.shape).astype(jnp.float32)
    soft = jnp.maximum(logits, 0.0) + jnp.log1p(jnp.exp(-jnp.abs(logits)))
    loss_ref[0] = jnp.sum(soft - label * logits)


def everyone(part, groups):
    return lax.all_to_all(part, ("row", "col"), 0, 0, axis_index_groups=groups, tiled=True)


def call(kernel, out_shape, name, *args, **more):
    return pl.pallas_call(kernel, out_shape=out_shape, name=name, **more, **params())(*args)


def merged(part, class_weight, slide_label):
    rest, shares = (jax.ShapeDtypeStruct((n, NQ // 8, 256), jnp.bfloat16) for n in (32, 16))
    parts = everyone(part.reshape(shares.shape), SHARES)
    parts = everyone(call(merge_kernel, rest, "merge_first", parts), REST)
    parts = everyone(call(merge_kernel, shares, "merge_second", parts), SHARES)
    return call(
        pool_kernel,
        (jax.ShapeDtypeStruct((NQ, WIDTH), jnp.float32), jax.ShapeDtypeStruct((1,), jnp.float32)),
        "pool",
        parts,
        class_weight.T,
        slide_label,
        out_specs=(pl.BlockSpec(memory_space=pltpu.VMEM), pl.BlockSpec(memory_space=pltpu.SMEM)),
    )


def vmem(*shape):
    return pltpu.VMEM(shape, jnp.float32)


def params(flops=1000000):
    return dict(
        compiler_params=pltpu.CompilerParams(vmem_limit_bytes=24 * 1024 * 1024),
        cost_estimate=pl.CostEstimate(flops=flops, bytes_accessed=1000000, transcendentals=0),
    )


def swapped(near, far, axis):
    count, odd = lax.axis_size(axis), lax.axis_index(axis) % 2 == 1
    inner = [(i, i ^ 1) for i in range(count)]
    outer = [(i, i + 1 if i % 2 else i - 1) for i in range(1, count - 1)]
    near, far = lax.ppermute(near, axis, inner), lax.ppermute(far, axis, outer)
    return jnp.where(odd, near, far), jnp.where(odd, far, near)


def exchanged(first, last, axis):
    odd = lax.axis_index(axis) % 2 == 1
    return swapped(jnp.where(odd, first, last), jnp.where(odd, last, first), axis)


def per_device(
    features,
    depth_weight,
    depth_bias,
    norm_gain,
    norm_bias,
    expand_weight,
    expand_bias,
    shrink_weight,
    shrink_bias,
    layer_scale,
    key_weight,
    value_weight,
    queries,
    class_weight,
    tissue,
    slide_label,
):
    rows, cols, width = features.shape
    f32, bf16 = jnp.float32, jnp.bfloat16
    hbm, whole = pl.BlockSpec(memory_space=pltpu.HBM), pl.BlockSpec(memory_space=pltpu.VMEM)
    shaped = jax.ShapeDtypeStruct
    cells, taps_, bias, near, far, first, last = call(
        fetch_kernel,
        (
            shaped(features.shape, bf16),
            shaped(depth_weight.shape, f32),
            shaped(depth_bias.shape, f32),
            *[shaped((3, cols, width), bf16)] * 2,
            *[shaped((rows, 3, width), bf16)] * 2,
        ),
        "fetch_cells",
        *(
            pltpu.with_memory_space_constraint(array, pltpu.HBM)
            for array in (features, depth_weight, depth_bias)
        ),
        in_specs=[hbm] * 3,
        out_specs=(whole,) * 7,
        scratch_shapes=[pltpu.SemaphoreType.DMA((3,))],
    )
    low, high = swapped(near, far, "row")
    acc, expand, query, lines = call(
        own_kernel,
        (
            shaped((rows, cols, width), f32),
            shaped(expand_weight.shape, bf16),
            shaped(queries.shape, bf16),
            shaped((16, width), f32),
        ),
        "own_cells",
        cells,
        taps_,
        bias,
        *(
            pltpu.with_memory_space_constraint(array, pltpu.HBM)
            for array in (
                expand_weight,
                queries,
                norm_gain,
                norm_bias,
                shrink_bias,
                layer_scale,
                expand_bias,
            )
        ),
        in_specs=[whole] * 3 + [hbm] * 7,
        out_specs=(whole,) * 4,
        scratch_shapes=[
            vmem(3 * cols // 8, rows, 24, LANES),
            *(vmem(width) for _ in range(4)),
            vmem(HID),
            pltpu.SemaphoreType.DMA((9,)),
        ],
    )
    first, last, acc = lax.optimization_barrier((first, last, acc))
    left, right = exchanged(
        jnp.concatenate([low[:, :3], first, high[:, :3]], axis=0),
        jnp.concatenate([low[:, -3:], last, high[:, -3:]], axis=0),
        "col",
    )
    count = rows * HALF
    work = [pltpu.VMEM((count, width), bf16), pltpu.VMEM((count, HID), bf16)]
    sides, inner, keys, values, shrink, key, turned, big = call(
        inner_kernel,
        (
            shaped((rows, HALF, width), f32),
            shaped((rows, HALF, width), bf16),
            shaped((count, width), bf16),
            shaped((width, count), bf16),
            shaped(shrink_weight.shape, bf16),
            shaped(key_weight.shape, bf16),
            shaped(value_weight.shape, bf16),
            shaped((width, NH * NQ), bf16),
        ),
        "inner_cells",
        acc,
        low,
        high,
        taps_,
        cells,
        lines,
        expand,
        *(
            pltpu.with_memory_space_constraint(array, pltpu.HBM)
            for array in (shrink_weight, key_weight, value_weight)
        ),
        query,
        in_specs=[whole] * 7 + [hbm] * 3 + [whole],
        out_specs=(whole,) * 8,
        scratch_shapes=[
            vmem(3, 6, cols + 16, LANES),
            vmem(rows, cols, width),
            *work,
            pltpu.VMEM(value_weight.shape, bf16),
            pltpu.SemaphoreType.DMA((6,)),
        ],
    )
    block_out, part = call(
        outer_kernel,
        (shaped((rows, cols, width), bf16), shaped((2, NQ, 256), bf16)),
        "outer_cells",
        tissue,
        sides,
        left,
        right,
        taps_,
        cells,
        lines,
        expand,
        shrink,
        key,
        turned,
        big,
        inner,
        keys,
        values,
        in_specs=[pl.BlockSpec(memory_space=pltpu.SMEM)] + [whole] * 14,
        out_specs=(hbm, whole),
        scratch_shapes=[
            vmem(rows, HALF, width),
            vmem(2, 3, rows + 6, 16, LANES),
            *work,
            vmem(width + LANES, LANES),
            pltpu.VMEM((rows, cols, width), bf16),
            pltpu.SemaphoreType.DMA,
        ],
    )
    pooled, slide_loss = merged(part, class_weight, slide_label)
    return (block_out, pooled, slide_loss)


def solution(mesh):
    placed = (P("row", "col", None),) + (P(),) * 13 + (P("row", "col"), P())
    return jax.shard_map(
        per_device,
        mesh=mesh,
        in_specs=placed,
        out_specs=(P("row", "col", None), P(), P()),
        check_vma=False,
    )
```

```python
import jax
import jax.numpy as jnp
from jax import lax
from jax.experimental import pallas as pl
from jax.experimental.pallas import tpu as pltpu
from jax.sharding import PartitionSpec as P

NH = 8
NQ = 64
TILE = 8
LOG2E = 1.4426950408889634


def device(z, near, y):
    return (z * 8 + near) * 8 + y


EIGHT, FOUR, TWO = range(8), range(4), range(2)
SHARES = [[device(2 * z + k, n, y) for k in TWO for n in EIGHT] for z in FOUR for y in EIGHT]
REST = [[device(2 * z + k, n, y) for z in FOUR for y in EIGHT] for k in TWO for n in EIGHT]
WIDTH = 384
LANES = 128
CELLS_R = 8
CELLS_C = 32
HID = 1536
HALF = 16
SHARE = 192
MARK = SHARE - LANES


def taps(acc, rows, weight_ref, lanes, b, first):
    for a in range(7):
        weight = weight_ref[a, b : b + 1, lanes]
        for i in range(CELLS_R):
            at = i + a - 3 - first
            if 0 <= at < len(rows):
                acc[i] = acc[i] + rows[at] * weight
    return acc


def fetch_kernel(
    x_hbm, weight_hbm, bias_hbm, x_ref, weight_ref, bias_ref, inner_ref, outer_ref, first_ref, last_ref, sems
):
    pairs = ((x_hbm, x_ref), (weight_hbm, weight_ref), (bias_hbm, bias_ref))
    copies = [pltpu.make_async_copy(s, d, sems.at[k]) for k, (s, d) in enumerate(pairs)]
    for copy in copies:
        copy.start()
    copies[0].wait()
    odd = lax.axis_index("row") % 2
    inner_ref[...] = x_ref[pl.ds((1 - odd) * (CELLS_R - 3), 3)]
    outer_ref[...] = x_ref[pl.ds(odd * (CELLS_R - 3), 3)]
    first_ref[...] = x_ref[:, 0:3, :]
    last_ref[...] = x_ref[:, CELLS_C - 3 : CELLS_C, :]
    for copy in copies[1:]:
        copy.wait()


def own_kernel(
    x_ref,
    weight_ref,
    bias_ref,
    query_hbm,
    gain_hbm,
    norm_bias_hbm,
    shrink_bias_hbm,
    scale_hbm,
    expand_bias_hbm,
    acc_ref,
    query_ref,
    rows_ref,
    wide,
    gain_ref,
    norm_bias_ref,
    shrink_bias_ref,
    scale_ref,
    expand_bias_ref,
    sems,
):
    pairs = (
        (gain_hbm, gain_ref),
        (norm_bias_hbm, norm_bias_ref),
        (shrink_bias_hbm, shrink_bias_ref),
        (scale_hbm, scale_ref),
        (expand_bias_hbm, expand_bias_ref),
        (query_hbm, query_ref),
    )
    copies = [pltpu.make_async_copy(s, d, sems.at[k]) for k, (s, d) in enumerate(pairs)]
    for copy in copies:
        copy.start()
    rows_ref[8:9, :] = bias_ref[...].reshape(1, WIDTH)
    groups = CELLS_C // 8
    for c in range(3):
        cells = x_ref[:, :, pl.ds(c * LANES, LANES)].astype(jnp.float32)
        for j in range(groups):
            for k in range(3):
                at = 8 * (j + k - 1)
                part = jnp.zeros((CELLS_R, 8, LANES), jnp.float32)
                if 0 <= at < CELLS_C:
                    part = cells[:, at : at + 8]
                wide[groups * c + j, :, 8 * k : 8 * k + 8, :] = part

    def lane_tile(step, carry):
        c, j = step // groups, step % groups
        lanes = pl.ds(pl.multiple_of(c * LANES, LANES), LANES)
        acc = [jnp.broadcast_to(rows_ref[8:9, lanes], (8, LANES))] * CELLS_R
        for b in range(7):
            rows = [wide[step, r, 5 + b : 13 + b, :] for r in range(CELLS_R)]
            acc = taps(acc, rows, weight_ref, lanes, b, 0)
        for i in range(CELLS_R):
            acc_ref[i, pl.ds(pl.multiple_of(8 * j, 8), 8), lanes] = acc[i]
        return carry

    lax.fori_loop(0, 3 * groups, lane_tile, 0)
    for copy in copies:
        copy.wait()
    for row, ref in enumerate((gain_ref, norm_bias_ref, shrink_bias_ref, scale_ref)):
        rows_ref[row : row + 1, :] = ref[...].reshape(1, WIDTH)
    for k in range(HID // WIDTH):
        rows_ref[4 + k : 5 + k, :] = expand_bias_ref[k * WIDTH : (k + 1) * WIDTH].reshape(1, WIDTH)


def halo_rows(acc_in, low_ref, high_ref, weight_ref, acc_ref, wide):
    for c in range(3):
        lanes = pl.ds(c * LANES, LANES)
        wide[c, :, 0:8, :] = jnp.zeros((6, 8, LANES), jnp.float32)
        wide[c, :, 8 + CELLS_C : 16 + CELLS_C, :] = jnp.zeros((6, 8, LANES), jnp.float32)
        wide[c, 0:3, 8 : 8 + CELLS_C, :] = low_ref[:, :, lanes].astype(jnp.float32)
        wide[c, 3:6, 8 : 8 + CELLS_C, :] = high_ref[:, :, lanes].astype(jnp.float32)

    def lane_tile(c, carry):
        lanes = pl.ds(pl.multiple_of(c * LANES, LANES), LANES)
        for j in range(CELLS_C // 8):
            acc = [acc_in[i, 8 * j : 8 * j + 8, lanes] for i in range(CELLS_R)]
            for b in range(7):
                at = 8 * j + 5 + b
                rows = [wide[c, r, at : at + 8, :] for r in range(6)]
                acc = taps(acc, rows[:3], weight_ref, lanes, b, -3)
                acc = taps(acc, rows[3:], weight_ref, lanes, b, CELLS_R)
            for i in range(CELLS_R):
                acc_ref[i, 8 * j : 8 * j + 8, lanes] = acc[i]
        return carry

    lax.fori_loop(0, 3, lane_tile, 0)


def halo_columns(acc_ref, left_ref, right_ref, weight_ref, edge):
    tall = CELLS_R + 6
    edge[...] = jnp.zeros(edge.shape, jnp.float32)
    for c in range(3):
        lanes = pl.ds(c * LANES, LANES)
        edge[0, c, :, 5:8, :] = left_ref[:, :, lanes].astype(jnp.float32)
        edge[1, c, :, 8:11, :] = right_ref[:, :, lanes].astype(jnp.float32)

    def lane_tile(c, carry):
        lanes = pl.ds(pl.multiple_of(c * LANES, LANES), LANES)
        for side in (0, 1):
            here = slice(8 * side, 8 * side + 8)
            acc = [acc_ref[i, here, lanes] for i in range(CELLS_R)]
            for b in (0, 1, 2) if side == 0 else (4, 5, 6):
                at = 5 + b if side == 0 else b - 3
                rows = [edge[side, c, r, at : at + 8, :] for r in range(tall)]
                acc = taps(acc, rows, weight_ref, lanes, b, -3)
            for i in range(CELLS_R):
                acc_ref[i, here, lanes] = acc[i]
        return carry

    lax.fori_loop(0, 3, lane_tile, 0)


def gelu(x):
    return 0.5 * x * (1.0 + lax.erf(x * (0.5**0.5)))


def block_of(conv_rows, inputs, lines_ref, expand_ref, shrink_ref, normed, hidden, copies=()):
    gain, norm_bias, shrink_bias, scale = (lines_ref[k : k + 1, :] for k in range(4))
    for i in range(CELLS_R):
        conv = conv_rows(i)
        center = jnp.mean(conv, axis=-1, keepdims=True)
        conv = conv - center
        variance = jnp.mean(conv * conv, axis=-1, keepdims=True)
        normed[i * HALF : (i + 1) * HALF, :] = (
            conv * lax.rsqrt(variance + 1e-06) * gain + norm_bias
        ).astype(jnp.bfloat16)
    for k in range(HID // WIDTH):
        lanes = slice(k * WIDTH, (k + 1) * WIDTH)
        part = jnp.dot(normed[...], expand_ref[:, lanes], preferred_element_type=jnp.float32)
        hidden[:, lanes] = gelu(part + lines_ref[4 + k : 5 + k, :]).astype(jnp.bfloat16)
    for copy in copies:
        copy.wait()
    shrunk = jnp.dot(hidden[...], shrink_ref[...], preferred_element_type=jnp.float32)
    shrunk = shrunk + shrink_bias
    inputs = inputs.reshape(CELLS_R * HALF, WIDTH).astype(jnp.float32)
    return (inputs + scale * shrunk).astype(jnp.bfloat16)


def keys_of(block, key_ref):
    return jnp.dot(block, key_ref[...], preferred_element_type=jnp.float32).astype(jnp.bfloat16)


def values_of(block, turned_ref):
    return lax.dot_general(
        turned_ref[...], block, (((1,), (1,)), ((), ())), preferred_element_type=jnp.float32
    ).astype(jnp.bfloat16)


def inner_kernel(
    acc_in,
    low_ref,
    high_ref,
    weight_ref,
    x_ref,
    lines_ref,
    expand_hbm,
    shrink_hbm,
    key_hbm,
    value_hbm,
    query_ref,
    sides_ref,
    block_ref,
    keys_ref,
    values_ref,
    expand_ref,
    shrink_ref,
    key_ref,
    turned_ref,
    big_ref,
    wide,
    acc_ref,
    normed,
    hidden,
    value_ref,
    sems,
):
    copies = [
        pltpu.make_async_copy(
            shrink_hbm.at[k * WIDTH : (k + 1) * WIDTH],
            shrink_ref.at[k * WIDTH : (k + 1) * WIDTH],
            sems.at[k],
        )
        for k in range(HID // WIDTH)
    ]
    late = [
        pltpu.make_async_copy(value_hbm, value_ref, sems.at[4]),
        pltpu.make_async_copy(key_hbm, key_ref, sems.at[5]),
    ]
    early = [
        pltpu.make_async_copy(
            expand_hbm.at[k * LANES : (k + 1) * LANES],
            expand_ref.at[k * LANES : (k + 1) * LANES],
            sems.at[6 + k],
        )
        for k in range(WIDTH // LANES)
    ]
    for copy in late[:1] + early + copies + late[1:]:
        copy.start()
    halo_rows(acc_in, low_ref, high_ref, weight_ref, acc_ref, wide)
    late[0].wait()
    turned_ref[...] = value_ref[...].astype(jnp.float32).T.astype(jnp.bfloat16)
    query = query_ref[...].astype(jnp.float32)
    query = jnp.concatenate([query, query], axis=0).T
    head = lax.broadcasted_iota(jnp.int32, (WIDTH, LANES), 0) // (WIDTH // NH)
    half = lax.broadcasted_iota(jnp.int32, (WIDTH, LANES), 1) // NQ
    for t in range(NH // 2):
        big_ref[:, t * LANES : (t + 1) * LANES] = jnp.where(
            head == 2 * t + half, query, 0.0
        ).astype(jnp.bfloat16)
    sides_ref[:, 0:8, :] = acc_ref[:, 0:8, :]
    sides_ref[:, 8:16, :] = acc_ref[:, CELLS_C - 8 : CELLS_C, :]
    for copy in early:
        copy.wait()
    block = block_of(
        lambda i: acc_ref[i, 8 : 8 + HALF, :],
        x_ref[:, 8 : 8 + HALF, :],
        lines_ref,
        expand_ref,
        shrink_ref,
        normed,
        hidden,
        copies,
    )
    block_ref[...] = block.reshape(CELLS_R, HALF, WIDTH)
    late[1].wait()
    keys_ref[...] = keys_of(block, key_ref)
    values_ref[...] = values_of(block, turned_ref)


def marked(weighted, marks):
    high = marks.astype(jnp.bfloat16).astype(jnp.float32)
    rest = marks - high
    middle = rest.astype(jnp.bfloat16).astype(jnp.float32)
    low = (rest - middle).astype(jnp.bfloat16).astype(jnp.float32)
    marks = high + pltpu.roll(middle, NH, 1) + pltpu.roll(low, 2 * NH, 1)
    lane = lax.broadcasted_iota(jnp.int32, marks.shape, 1)
    last = jnp.where(lane < MARK, weighted[:, LANES:], marks)
    return jnp.concatenate([weighted[:, :LANES], last], axis=1).astype(jnp.bfloat16)


def outer_kernel(
    tissue_ref,
    acc_in,
    left_ref,
    right_ref,
    weight_ref,
    x_ref,
    lines_ref,
    expand_ref,
    shrink_ref,
    key_ref,
    turned_ref,
    big_ref,
    block_ref,
    keys_ref,
    values_ref,
    out_ref,
    part_ref,
    acc_ref,
    edge,
    normed,
    hidden,
    sums,
    whole,
    sem,
):
    acc_ref[...] = acc_in[...]
    whole[:, 8 : 8 + HALF, :] = block_ref[...]
    halo_columns(acc_ref, left_ref, right_ref, weight_ref, edge)
    block = block_of(
        lambda i: acc_ref[i],
        jnp.concatenate([x_ref[:, 0:8, :], x_ref[:, CELLS_C - 8 : CELLS_C, :]], axis=1),
        lines_ref,
        expand_ref,
        shrink_ref,
        normed,
        hidden,
    )
    parts = block.reshape(CELLS_R, HALF, WIDTH)
    whole[:, 0:8, :] = parts[:, 0:8, :]
    whole[:, CELLS_C - 8 : CELLS_C, :] = parts[:, 8:16, :]
    copy = pltpu.make_async_copy(whole, out_ref, sem)
    copy.start()
    keys = jnp.concatenate([keys_ref[...], keys_of(block, key_ref)], axis=0)
    values = jnp.concatenate([values_ref[...], values_of(block, turned_ref)], axis=1)
    size = WIDTH // NH
    tiles = ((1, 2), (0, 3))
    live = [[tissue_ref[0, t] > 0 for t in pair] for pair in tiles]
    line = lax.broadcasted_iota(jnp.int32, (NH, LANES), 0)
    tops = jnp.zeros((NH, LANES), jnp.float32)
    totals = jnp.zeros((NH, LANES), jnp.float32)
    scores = jnp.dot(keys, big_ref[...], preferred_element_type=jnp.float32)
    scores = (scores * (size**-0.5 * LOG2E)).reshape(2, CELLS_R, 2, TILE, NH * NQ)
    scores = [[jnp.where(live[h][g], scores[h, :, g], -1e30) for g in range(2)] for h in range(2)]
    all_top = jnp.maximum(
        jnp.maximum(scores[0][0], scores[0][1]), jnp.maximum(scores[1][0], scores[1][1])
    )
    all_top = jnp.ceil(jnp.max(jnp.max(all_top, axis=0), axis=0, keepdims=True))
    weights = [
        [jnp.where(live[h][g], jnp.exp2(scores[h][g] - all_top), 0.0) for g in range(2)]
        for h in range(2)
    ]
    all_total = (weights[0][0] + weights[0][1]) + (weights[1][0] + weights[1][1])
    all_total = jnp.sum(jnp.sum(all_total, axis=0), axis=0, keepdims=True)
    weights = [jnp.stack(pair, axis=1).reshape(CELLS_R * HALF, NH * NQ) for pair in weights]
    weights = jnp.concatenate(weights, axis=0).astype(jnp.bfloat16)
    for t in range(NH // 2):
        lanes = slice(t * LANES, (t + 1) * LANES)
        top, total = all_top[:, lanes], all_total[:, lanes]
        pair = jnp.dot(
            values[2 * size * t : 2 * size * (t + 1), :],
            weights[:, lanes],
            preferred_element_type=jnp.float32,
        )
        at = 2 * size * t + (t // 2) * (256 - SHARE)
        sums[at : at + size, :] = pair[:size]
        sums[at + size : at + 2 * size, :] = pltpu.roll(pair[size:], NQ, 1)
        top = jnp.broadcast_to(top, (NH, LANES))
        total = jnp.broadcast_to(total, (NH, LANES))
        tops = jnp.where(line == 2 * t, top, tops)
        tops = jnp.where(line == 2 * t + 1, pltpu.roll(top, NQ, 1), tops)
        totals = jnp.where(line == 2 * t, total, totals)
        totals = jnp.where(line == 2 * t + 1, pltpu.roll(total, NQ, 1), totals)
    for u in range(2):
        at = 256 * u + SHARE
        sums[at : at + 64, :] = jnp.zeros((64, LANES), jnp.float32)
        sums[at : at + NH, :] = pltpu.roll(tops, 4, 0) if u else tops
        sums[at + 3 * NH : at + 4 * NH, :] = pltpu.roll(totals, 4, 0) if u else totals
    part = sums[...].T
    for u in range(2):
        share = part[:NQ, 256 * u : 256 * (u + 1)]
        lane = lax.broadcasted_iota(jnp.int32, (NQ, LANES), 1)
        part_ref[u] = marked(share, jnp.where(lane < MARK, 0.0, share[:, LANES:]))
    copy.wait()


def spread_matrix(first, copies):
    lane = lax.broadcasted_iota(jnp.int32, (LANES, 256), 0) - first
    head = lax.broadcasted_iota(jnp.int32, (LANES, 256), 1) // (WIDTH // NH)
    inside = (lane >= 0) & (lane < copies * NH) & (head < 4)
    return jnp.where(inside & (lane % NH == head), 1.0, 0.0).astype(jnp.bfloat16)


def merge_kernel(parts_ref, out_ref):
    n, q, width = parts_ref.shape
    parts = parts_ref[...].astype(jnp.float32)
    lane = lax.broadcasted_iota(jnp.int32, (n * q, LANES), 1)
    marks = parts[:, :, LANES:].reshape(n * q, LANES)
    marks = jnp.where(lane < MARK, 0.0, marks)
    marks = marks + pltpu.roll(marks, LANES - NH, 1) + pltpu.roll(marks, LANES - 2 * NH, 1)
    top = jnp.max(marks.reshape(n, q, LANES), axis=0)
    factor = jnp.exp2(marks.reshape(n, q, LANES) - top).reshape(n * q, LANES)
    factor = factor.astype(jnp.bfloat16)
    spread = jnp.dot(factor, spread_matrix(MARK, 1), preferred_element_type=jnp.float32)
    weighted = jnp.sum(parts * spread.reshape(n, q, width), axis=0)
    total = marks * pltpu.roll(factor.astype(jnp.float32), 3 * NH, 1)
    total = jnp.sum(total.reshape(n, q, LANES), axis=0)
    lane = lane[:q]
    part = jnp.where((lane >= MARK) & (lane < MARK + 4), top, 0.0)
    part = jnp.where((lane >= MARK + 3 * NH) & (lane < MARK + 3 * NH + 4), total, part)
    share = marked(weighted, part)
    out_ref[...] = jnp.broadcast_to(share[None], out_ref.shape)


def pool_kernel(parts_ref, class_ref, label_ref, out_ref, loss_ref):
    parts = parts_ref[...].reshape(2 * NQ, 256).astype(jnp.float32)
    lane = lax.broadcasted_iota(jnp.int32, (2 * NQ, LANES), 1)
    first = MARK + 3 * NH
    marks = jnp.where(lane < MARK, 0.0, parts[:, LANES:])
    marks = marks + pltpu.roll(marks, LANES - NH, 1) + pltpu.roll(marks, LANES - 2 * NH, 1)
    inside = (lane >= first) & (lane < first + 4)
    marks = jnp.where(inside, 1.0 / jnp.where(inside, marks, 1.0), 0.0)
    marks = marked(parts, marks)[:, LANES:]
    inverse = jnp.dot(marks, spread_matrix(first, 3), preferred_element_type=jnp.float32)
    pooled = (parts * inverse).reshape(2, NQ, 256)
    pooled = jnp.concatenate([pooled[0, :, :SHARE], pooled[1, :, :SHARE]], axis=1)
    out_ref[...] = pooled
    lines = jnp.sum(pooled.reshape(NQ // 8, 8, WIDTH), axis=0)
    logits = lax.dot_general(
        lines,
        class_ref[...],
        (((1,), (1,)), ((), ())),
        precision=lax.Precision.HIGHEST,
        preferred_element_type=jnp.float32,
    )
    logits = jnp.sum(logits, axis=0, keepdims=True)
    label = label_ref[...].reshape(logits.shape).astype(jnp.float32)
    soft = jnp.maximum(logits, 0.0) + jnp.log1p(jnp.exp(-jnp.abs(logits)))
    loss_ref[0] = jnp.sum(soft - label * logits)


def everyone(part, groups):
    return lax.all_to_all(part, ("row", "col"), 0, 0, axis_index_groups=groups, tiled=True)


def call(kernel, out_shape, name, *args, **more):
    return pl.pallas_call(kernel, out_shape=out_shape, name=name, **more, **params())(*args)


def merged(part, class_weight, slide_label):
    rest, shares = (jax.ShapeDtypeStruct((n, NQ // 8, 256), jnp.bfloat16) for n in (32, 16))
    parts = everyone(part.reshape(shares.shape), SHARES)
    parts = everyone(call(merge_kernel, rest, "merge_first", parts), REST)
    parts = everyone(call(merge_kernel, shares, "merge_second", parts), SHARES)
    return call(
        pool_kernel,
        (jax.ShapeDtypeStruct((NQ, WIDTH), jnp.float32), jax.ShapeDtypeStruct((1,), jnp.float32)),
        "pool",
        parts,
        class_weight.T,
        slide_label,
        out_specs=(pl.BlockSpec(memory_space=pltpu.VMEM), pl.BlockSpec(memory_space=pltpu.SMEM)),
    )


def vmem(*shape):
    return pltpu.VMEM(shape, jnp.float32)


def params(flops=1000000):
    return dict(
        compiler_params=pltpu.CompilerParams(vmem_limit_bytes=24 * 1024 * 1024),
        cost_estimate=pl.CostEstimate(flops=flops, bytes_accessed=1000000, transcendentals=0),
    )


def swapped(near, far, axis):
    count, odd = lax.axis_size(axis), lax.axis_index(axis) % 2 == 1
    inner = [(i, i ^ 1) for i in range(count)]
    outer = [(i, i + 1 if i % 2 else i - 1) for i in range(1, count - 1)]
    near, far = lax.ppermute(near, axis, inner), lax.ppermute(far, axis, outer)
    return jnp.where(odd, near, far), jnp.where(odd, far, near)


def exchanged(first, last, axis):
    odd = lax.axis_index(axis) % 2 == 1
    return swapped(jnp.where(odd, first, last), jnp.where(odd, last, first), axis)


def per_device(
    features,
    depth_weight,
    depth_bias,
    norm_gain,
    norm_bias,
    expand_weight,
    expand_bias,
    shrink_weight,
    shrink_bias,
    layer_scale,
    key_weight,
    value_weight,
    queries,
    class_weight,
    tissue,
    slide_label,
):
    rows, cols, width = features.shape
    f32, bf16 = jnp.float32, jnp.bfloat16
    hbm, whole = pl.BlockSpec(memory_space=pltpu.HBM), pl.BlockSpec(memory_space=pltpu.VMEM)
    shaped = jax.ShapeDtypeStruct
    cells, taps_, bias, near, far, first, last = call(
        fetch_kernel,
        (
            shaped(features.shape, bf16),
            shaped(depth_weight.shape, f32),
            shaped(depth_bias.shape, f32),
            *[shaped((3, cols, width), bf16)] * 2,
            *[shaped((rows, 3, width), bf16)] * 2,
        ),
        "fetch_cells",
        *(
            pltpu.with_memory_space_constraint(array, pltpu.HBM)
            for array in (features, depth_weight, depth_bias)
        ),
        in_specs=[hbm] * 3,
        out_specs=(whole,) * 7,
        scratch_shapes=[pltpu.SemaphoreType.DMA((3,))],
    )
    low, high = swapped(near, far, "row")
    acc, query, lines = call(
        own_kernel,
        (
            shaped((rows, cols, width), f32),
            shaped(queries.shape, bf16),
            shaped((16, width), f32),
        ),
        "own_cells",
        cells,
        taps_,
        bias,
        *(
            pltpu.with_memory_space_constraint(array, pltpu.HBM)
            for array in (
                queries,
                norm_gain,
                norm_bias,
                shrink_bias,
                layer_scale,
                expand_bias,
            )
        ),
        in_specs=[whole] * 3 + [hbm] * 6,
        out_specs=(whole,) * 3,
        scratch_shapes=[
            vmem(3 * cols // 8, rows, 24, LANES),
            *(vmem(width) for _ in range(4)),
            vmem(HID),
            pltpu.SemaphoreType.DMA((6,)),
        ],
    )
    first, last, acc = lax.optimization_barrier((first, last, acc))
    left, right = exchanged(
        jnp.concatenate([low[:, :3], first, high[:, :3]], axis=0),
        jnp.concatenate([low[:, -3:], last, high[:, -3:]], axis=0),
        "col",
    )
    count = rows * HALF
    work = [pltpu.VMEM((count, width), bf16), pltpu.VMEM((count, HID), bf16)]
    sides, inner, keys, values, expand, shrink, key, turned, big = call(
        inner_kernel,
        (
            shaped((rows, HALF, width), f32),
            shaped((rows, HALF, width), bf16),
            shaped((count, width), bf16),
            shaped((width, count), bf16),
            shaped(expand_weight.shape, bf16),
            shaped(shrink_weight.shape, bf16),
            shaped(key_weight.shape, bf16),
            shaped(value_weight.shape, bf16),
            shaped((width, NH * NQ), bf16),
        ),
        "inner_cells",
        acc,
        low,
        high,
        taps_,
        cells,
        lines,
        *(
            pltpu.with_memory_space_constraint(array, pltpu.HBM)
            for array in (expand_weight, shrink_weight, key_weight, value_weight)
        ),
        query,
        in_specs=[whole] * 6 + [hbm] * 4 + [whole],
        out_specs=(whole,) * 9,
        scratch_shapes=[
            vmem(3, 6, cols + 16, LANES),
            vmem(rows, cols, width),
            *work,
            pltpu.VMEM(value_weight.shape, bf16),
            pltpu.SemaphoreType.DMA((9,)),
        ],
    )
    block_out, part = call(
        outer_kernel,
        (shaped((rows, cols, width), bf16), shaped((2, NQ, 256), bf16)),
        "outer_cells",
        tissue,
        sides,
        left,
        right,
        taps_,
        cells,
        lines,
        expand,
        shrink,
        key,
        turned,
        big,
        inner,
        keys,
        values,
        in_specs=[pl.BlockSpec(memory_space=pltpu.SMEM)] + [whole] * 14,
        out_specs=(hbm, whole),
        scratch_shapes=[
            vmem(rows, HALF, width),
            vmem(2, 3, rows + 6, 16, LANES),
            *work,
            vmem(width + LANES, LANES),
            pltpu.VMEM((rows, cols, width), bf16),
            pltpu.SemaphoreType.DMA,
        ],
    )
    pooled, slide_loss = merged(part, class_weight, slide_label)
    return (block_out, pooled, slide_loss)


def solution(mesh):
    placed = (P("row", "col", None),) + (P(),) * 13 + (P("row", "col"), P())
    return jax.shard_map(
        per_device,
        mesh=mesh,
        in_specs=placed,
        out_specs=(P("row", "col", None), P(), P()),
        check_vma=False,
    )
```
